32 devices in a mesh: group: 2 (over y), visit: 16 (over z, x, core), sky: 1.
Axes of the slice: x: 2, y: 2, z: 4, core: 2. Of those that a mesh axis runs over, the one named last changes fastest.
Arguments:
- template: bfloat16 [64, 128], P(('group', 'visit'), 'sky'), parts along dimension 0, may hold values from -6 to 6
- science: float32 [32, 32, 128], P(('group', 'visit'), None, 'sky'), parts along dimension 0, may hold values from -15 to 15
- variance: float32 [32, 32, 128], P(('group', 'visit'), None, 'sky'), parts along dimension 0, may hold values from 0.5 to 4
- col_taps: bfloat16 [49, 31], replicated, may hold values from -1 to 1
- row_taps: bfloat16 [49, 31], replicated, may hold values from -1 to 1
- stamp_rows: int32 [32, 1, 16], P(('group', 'visit'), 'sky'), parts along dimension 0, may hold values from 0 to 16
- stamp_cols: int32 [32, 1, 16], P(('group', 'visit'), 'sky'), parts along dimension 0, may hold values from 0 to 112
Outputs:
- difference: float32 [32, 32, 128], P(('group', 'visit'), None, 'sky'), parts along dimension 0
- coefficients: float32 [32, 50], P(('group', 'visit')), parts along dimension 0
- detection: float32 [64, 128], P(('group', 'visit'), 'sky'), parts along dimension 0
The draws below stay inside these ranges and needn't reach their ends.
There are 2 independent parts, one for each index of `group`. The reference program is written for one: setup_inputs(seed, part) draws one part's arguments, and reference() takes and returns one part's arrays. A program takes and returns all parts, laid end to end along the dimension named above; an argument that names none is the same for every part. Nothing has to cross between parts.
All inputs are finite; a program needn't handle non-finite values.
Results may differ from the reference program's by a relative error of at most 0.0018.
Values may be sent and summed in bfloat16 or wider, within the bound.
A program may use at most 128 MiB of HBM per device.

```python
import math
import jax
import jax.numpy as jnp
from jax import lax

NB = 49
TAPS = 31
STAMP = 16
STAMPS = 16
TILE_W = 128
TILE_H = 32
VISITS = 16
SKY_TILES = 1
PATCH_W = 128


def shared_field(key):
    base_field = jax.random.normal(jax.random.fold_in(key, 101), (TILE_H, PATCH_W), jnp.float32)
    return jnp.clip(base_field, -6.0, 6.0)


def draw_template(key, part):
    return shared_field(key).astype(jnp.bfloat16)


def draw_science(key, part):
    base_field = shared_field(key)
    visit_gains = jax.random.uniform(jax.random.fold_in(key, 202), (VISITS, 1, 1), jnp.float32, 0.5, 2.0)
    raw_noise = jax.random.normal(jax.random.fold_in(key, 303), (VISITS, TILE_H, PATCH_W), jnp.float32)
    noise_field = 0.5 * jnp.clip(raw_noise, -6.0, 6.0)
    return visit_gains * base_field[None, :, :] + noise_field


def plant(array, stream_key, low, top_value):
    longest = array.shape.index(max(array.shape))
    spots = []
    for shift in (0, 1):
        where = [jax.random.randint(jax.random.fold_in(stream_key, axis), (), 0, length) for axis, length in enumerate(array.shape)]
        where[longest] = (where[longest] + shift) % array.shape[longest]
        spots.append(tuple(where))
    return array.at[spots[0]].set(low).at[spots[1]].set(top_value)


def block_scale(own_key, dims, pieces, low, top_value):
    def one(dim, shards_of):
        heights = jax.random.uniform(jax.random.fold_in(jax.random.fold_in(own_key, 6), dim), (shards_of,), jnp.float32, low / len(pieces), top_value / len(pieces))
        return jnp.repeat(jnp.exp(heights), dims[dim] // shards_of).reshape((-1,) + (1,) * (len(dims) - dim - 1))

    factor_of = one(*pieces[0])
    for cut in pieces[1:]:
        factor_of = factor_of * one(*cut)
    return factor_of


def bell_draw(own_key, shape, spread, bound, held_as=jnp.bfloat16):
    entries = jax.random.normal(own_key, shape, jnp.float32) * spread
    return jnp.minimum(jnp.maximum(entries, -bound), bound).astype(held_as)


def setup_inputs(seed: int = 0, part: int = 0) -> dict:
    splits = jax.random.split(jax.random.key(seed), 8)
    part_splits = jax.random.split(jax.random.fold_in(splits[7], part), 8)
    template = draw_template(jax.random.fold_in(jax.random.fold_in(splits[7], part), 71), part)
    science = draw_science(jax.random.fold_in(jax.random.fold_in(splits[7], part), 71), part)
    variance = jnp.clip(jnp.exp(math.log(4.0) - 2.0794415 * jax.random.uniform(part_splits[2], (VISITS, TILE_H, PATCH_W), jnp.float32) ** block_scale(part_splits[2], (VISITS, TILE_H, PATCH_W), ((0, 16),), -0.2, 0.2)), 0.5, 4.0)
    col_taps = bell_draw(splits[3], (NB, TAPS), TAPS ** -0.5, 1.0)
    row_taps = bell_draw(splits[4], (NB, TAPS), TAPS ** -0.5, 1.0)
    stamp_rows = plant(jax.random.randint(part_splits[5], (VISITS, SKY_TILES, STAMPS), 0, TILE_H - STAMP + 1), jax.random.fold_in(part_splits[5], 1), 0, TILE_H - STAMP).astype(jnp.int32)
    stamp_cols = plant(jax.random.randint(part_splits[6], (VISITS, SKY_TILES, STAMPS), 0, TILE_W - STAMP + 1), jax.random.fold_in(part_splits[6], 1), 0, TILE_W - STAMP).astype(jnp.int32)
    return {"template": template, "science": science, "variance": variance, "col_taps": col_taps, "row_taps": row_taps, "stamp_rows": stamp_rows, "stamp_cols": stamp_cols}


def column_pass(padded, taps):
    out_width = padded.shape[1] - TAPS + 1
    shifted = jnp.stack([padded[:, offset:offset + out_width] for offset in range(TAPS)]).astype(jnp.float32)
    result = jnp.einsum('kj,jhw->khw', taps.astype(jnp.float32), shifted, precision=lax.Precision.HIGHEST)
    return result.astype(jnp.bfloat16)

def row_pass(columns, taps):
    margin = (TAPS - 1) // 2
    height = columns.shape[1]
    padded = jnp.pad(columns.astype(jnp.float32), ((0, 0), (margin, margin), (0, 0)))
    total = jnp.zeros(columns.shape, jnp.float32)
    for offset in range(TAPS):
        total = total + taps[:, offset].astype(jnp.float32)[:, None, None] * padded[:, offset:offset + height, :]
    return total.astype(jnp.bfloat16)

def cholesky_solve(matrix, vector):
    factor = jnp.linalg.cholesky(matrix)
    middle = lax.linalg.triangular_solve(factor, vector[:, None], left_side=True, lower=True)
    answer = lax.linalg.triangular_solve(factor, middle, left_side=True, lower=True, transpose_a=True)
    return answer[:, 0]

def reference(template, science, variance, col_taps, row_taps, stamp_rows, stamp_cols):
    margin = (TAPS - 1) // 2
    padded = jnp.pad(template, ((0, 0), (margin, margin)))
    columns = column_pass(padded, col_taps)
    convolved = row_pass(columns, row_taps)
    convolved_wide = convolved.astype(jnp.float32)
    shifts = (jnp.arange(SKY_TILES, dtype=jnp.int32) * TILE_W)[None, :, None]
    col_starts = (stamp_cols + shifts).reshape(VISITS, -1)
    row_starts = stamp_rows.reshape(VISITS, -1)

    def one_visit(inputs):
        science_map, variance_map, rows_here, cols_here = inputs

        def extract(row_start, col_start):
            block = lax.dynamic_slice(convolved, (jnp.int32(0), row_start, col_start), (NB, STAMP, STAMP))
            values = lax.dynamic_slice(science_map, (row_start, col_start), (STAMP, STAMP))
            noises = lax.dynamic_slice(variance_map, (row_start, col_start), (STAMP, STAMP))
            return (block, values, noises)
        blocks, values, noises = jax.vmap(extract)(rows_here, cols_here)
        design_core = jnp.transpose(blocks, (1, 0, 2, 3)).reshape(NB, -1)
        design = jnp.concatenate([design_core, jnp.ones((1, design_core.shape[1]), design_core.dtype)], axis=0).astype(jnp.float32)
        weights = 1.0 / noises.reshape(-1)
        normal = jnp.dot(design * weights[None, :], design.T, precision=lax.Precision.HIGHEST)
        target = jnp.dot(design, weights * values.reshape(-1), precision=lax.Precision.HIGHEST)
        solution = cholesky_solve(normal, target)
        model_map = jnp.tensordot(solution[:NB], convolved_wide, axes=1, precision=lax.Precision.HIGHEST)
        residual = science_map - model_map - solution[NB]
        return (residual / jnp.sqrt(variance_map), solution, residual / variance_map)
    differences, solutions, weighted = lax.map(one_visit, (science, variance, row_starts, col_starts))
    detection = lax.optimization_barrier(jnp.sum(weighted, axis=0)) / jnp.sqrt(lax.optimization_barrier(jnp.sum(1.0 / variance, axis=0)))
    return (differences, solutions, detection)
```

```python
import functools

import jax
import jax.numpy as jnp
from jax import lax
from jax.experimental import pallas as pl
from jax.experimental.pallas import tpu as pltpu
from jax.sharding import PartitionSpec as P

KBLK = 7
STAMP = 16


def with_halo(cells, sides, width):
    for axis, dim in sides:
        count = lax.axis_size(axis)
        ends = count - 1
        head = lax.slice_in_dim(cells, 0, width, axis=dim)
        tail = lax.slice_in_dim(cells, cells.shape[dim] - width, cells.shape[dim], axis=dim)
        cells = jnp.concatenate(
            [
                lax.ppermute(tail, axis, [(i, (i + 1) % count) for i in range(ends)]),
                cells,
                lax.ppermute(head, axis, [((i + 1) % count, i) for i in range(ends)]),
            ],
            axis=dim,
        )
    return cells


def tap_selectors(out_len, in_len, tap_count):
    offsets = (
        jnp.arange(in_len, dtype=jnp.int32)[None, :] - jnp.arange(out_len, dtype=jnp.int32)[:, None]
    )
    return (offsets[None, :, :] == jnp.arange(tap_count, dtype=jnp.int32)[:, None, None]).astype(
        jnp.float32
    )


def column_pass(padded, taps_block):
    tap_count = taps_block.shape[1]
    out_width = padded.shape[1] - tap_count + 1
    selectors = tap_selectors(out_width, padded.shape[1], tap_count)
    band_mats = jnp.einsum("kj,jci->kic", taps_block.astype(jnp.float32), selectors).astype(
        jnp.bfloat16
    )
    result = jnp.einsum("ri,kic->krc", padded, band_mats, preferred_element_type=jnp.float32)
    return result.astype(jnp.bfloat16)


def band_matrix(taps_block, out_len, in_len):
    tap_count = taps_block.shape[1]
    offsets = (
        jnp.arange(in_len, dtype=jnp.int32)[None, :] - jnp.arange(out_len, dtype=jnp.int32)[:, None]
    )
    taps_wide = taps_block.astype(jnp.float32)
    band = jnp.zeros((taps_block.shape[0], out_len, in_len), jnp.float32)
    for offset in range(tap_count):
        band = band + jnp.where(
            offsets[None, :, :] == offset, taps_wide[:, offset][:, None, None], 0.0
        )
    return band.astype(jnp.bfloat16)


def row_pass(columns, taps_block):
    tap_count = taps_block.shape[1]
    margin = (tap_count - 1) // 2
    height = columns.shape[1]
    stride = min(512, height)
    padded = jnp.pad(columns, ((0, 0), (margin, margin), (0, 0)))
    band = band_matrix(taps_block, stride, stride + 2 * margin)
    pieces = jnp.einsum("kti,kiw->ktw", band, padded, preferred_element_type=jnp.float32).astype(
        jnp.bfloat16
    )
    return pieces


def extract_stamps(block, row_starts, col_starts):

    def extract(row_start, col_start):
        return lax.dynamic_slice(
            block, (jnp.int32(0), row_start, col_start), (block.shape[0], STAMP, STAMP)
        )

    stamps = jax.vmap(extract)(row_starts, col_starts)
    return jnp.transpose(stamps, (1, 0, 2, 3)).reshape(block.shape[0], -1)


def extract_plane(plane, row_starts, col_starts):

    def extract(row_start, col_start):
        return lax.dynamic_slice(plane, (row_start, col_start), (STAMP, STAMP))

    return jax.vmap(extract)(row_starts, col_starts).reshape(-1)


def cholesky_solve(matrix, vector):
    factor = jnp.linalg.cholesky(matrix)
    middle = lax.linalg.triangular_solve(factor, vector[:, None], left_side=True, lower=True)
    answer = lax.linalg.triangular_solve(
        factor, middle, left_side=True, lower=True, transpose_a=True
    )
    return answer[:, 0]


def on_device(template, science, variance, col_taps, row_taps, stamp_rows, stamp_cols):
    tap_count = col_taps.shape[1]
    margin = (tap_count - 1) // 2
    kernels = col_taps.shape[0]
    blocks = kernels // KBLK
    science_map = science[0]
    variance_map = variance[0]
    inverse = 1.0 / variance_map
    gathered = lax.all_gather(template, "visit", axis=0, tiled=True)
    padded_tile = with_halo(gathered, (("sky", 1),), margin)
    image_list = []
    for block_index in range(blocks):
        image_list.append(
            row_pass(
                column_pass(padded_tile, col_taps[block_index * KBLK : (block_index + 1) * KBLK]),
                row_taps[block_index * KBLK : (block_index + 1) * KBLK],
            )
        )
    convolved = jnp.concatenate(image_list, axis=0)
    row_starts = stamp_rows[0, 0]
    col_starts = stamp_cols[0, 0]
    design_core = extract_stamps(convolved, row_starts, col_starts)
    design = jnp.concatenate(
        [design_core, jnp.ones((1, design_core.shape[1]), design_core.dtype)], axis=0
    ).astype(jnp.float32)
    weights = 1.0 / extract_plane(variance_map, row_starts, col_starts)
    values = extract_plane(science_map, row_starts, col_starts)
    partial_normal = jnp.dot(design * weights[None, :], design.T, precision=lax.Precision.HIGHEST)
    partial_target = jnp.dot(design, weights * values, precision=lax.Precision.HIGHEST)
    normal, target = lax.psum((partial_normal, partial_target), "sky")
    solution = cholesky_solve(normal, target)

    def model_step(block_index, total):
        images = lax.dynamic_slice_in_dim(convolved, block_index * KBLK, KBLK, 0).astype(
            jnp.float32
        )
        share = lax.dynamic_slice_in_dim(solution, block_index * KBLK, KBLK, 0)
        return total + jnp.tensordot(share, images, axes=1, precision=lax.Precision.HIGHEST)

    model_map = lax.fori_loop(0, blocks, model_step, jnp.zeros(science_map.shape, jnp.float32))
    residual = science_map - model_map - solution[kernels]
    difference = (residual / jnp.sqrt(variance_map))[None, :, :]
    weighted = residual / variance_map
    numerator, weight_total = (
        lax.psum_scatter(weighted, "visit", scatter_dimension=0, tiled=True),
        lax.psum_scatter(inverse, "visit", scatter_dimension=0, tiled=True),
    )
    detection = numerator / jnp.sqrt(weight_total)
    return (difference, solution[None, :], detection)


MESH = pl.DeviceIdType.MESH
SUB = 8
EXTRA = 4


def dot(a, b, contract=((1,), (0,))):
    return lax.dot_general(a, b, (contract, ((), ())), preferred_element_type=jnp.float32)


def split3(value):
    high = value.astype(jnp.bfloat16)
    rest = value - high.astype(jnp.float32)
    middle = rest.astype(jnp.bfloat16)
    low = (rest - middle.astype(jnp.float32)).astype(jnp.bfloat16)
    return high, middle, low


def iota(shape, dim):
    return lax.broadcasted_iota(jnp.int32, shape, dim)


def placed_taps(taps, lanes, sign):
    count = taps.shape[1]
    margin = (count - 1) // 2
    spot = sign * (iota((count, lanes), 0) - margin)
    spot = jnp.where(spot < 0, spot + lanes, spot)
    place = jnp.where(iota((count, lanes), 1) == spot, 1.0, 0.0).astype(jnp.bfloat16)
    return dot(taps, place)


def fused_kernel(
    n,
    template_ref,
    science_ref,
    variance_ref,
    col_taps_ref,
    row_taps_ref,
    stamp_rows_ref,
    stamp_cols_ref,
    difference_ref,
    coefficients_ref,
    detection_ref,
    outbox,
    inbox,
    parts_out,
    parts_in,
    tile,
    col_bands,
    row_bands,
    design,
    send_a,
    recv_a,
    send_b,
    recv_b,
):
    me = lax.axis_index("visit")
    kernels, taps = col_taps_ref.shape
    margin = (taps - 1) // 2
    share, width = template_ref.shape
    height = science_ref.shape[1]
    groups = row_bands.shape[0]
    stacked = SUB * height

    def copies(source, target, send, recv):
        return [
            pltpu.make_async_remote_copy(
                src_ref=source.at[lax.rem(me + step, n)],
                dst_ref=target.at[me],
                send_sem=send.at[step],
                recv_sem=recv.at[step],
                device_id={"visit": lax.rem(me + step, n)},
                device_id_type=MESH,
            )
            for step in range(1, n)
        ]

    barrier = pltpu.get_barrier_semaphore()
    for step in range(1, n):
        pl.semaphore_signal(
            barrier, inc=1, device_id={"visit": lax.rem(me + step, n)}, device_id_type=MESH
        )

    science = science_ref[0]
    variance = variance_ref[0]
    inverse = 1.0 / variance
    own_rows = template_ref[...].astype(jnp.float32)
    for owner in range(n):
        outbox[owner, 0:share, :] = own_rows
        outbox[owner, share : 2 * share, :] = inverse[owner * share : (owner + 1) * share]
    inbox[me] = outbox[me]

    spread = placed_taps(row_taps_ref[...], stacked, 1)
    spread = jnp.concatenate(
        [spread, jnp.zeros((groups * SUB - kernels, stacked), jnp.float32)], axis=0
    )
    own_block = iota((SUB, stacked), 1) // height == iota((SUB, stacked), 0)
    for group in range(groups):
        source = spread[group * SUB : (group + 1) * SUB]
        base = source
        for sub in range(1, SUB):
            base = jnp.where(
                iota((SUB, stacked), 0) == sub, pltpu.roll(source, sub * height, 1), base
            )
        for row in range(0, height, 2):
            pair = [
                jnp.where(own_block, pltpu.roll(base, row + more, 1), 0.0) for more in range(2)
            ]
            row_bands[group, row * SUB : (row + 2) * SUB, :] = jnp.concatenate(
                pair, axis=0
            ).astype(jnp.bfloat16)

    pl.semaphore_wait(barrier, n - 1)
    first = copies(outbox, inbox, send_a, recv_a)
    for copy in first:
        copy.start()

    lanes = placed_taps(col_taps_ref[...], width, -1)
    near = jnp.abs(iota((width, width), 0) - iota((width, width), 1)) <= margin
    for k in range(kernels):
        base = pltpu.roll(
            jnp.broadcast_to(lanes[k : k + 1], (width, width)), 0, 1, stride=1, stride_axis=0
        )
        col_bands[:, k * width : (k + 1) * width] = jnp.where(near, base, 0.0).astype(jnp.bfloat16)

    tops = stamp_rows_ref[0]
    lefts = stamp_cols_ref[0]
    down = iota((height, tops.shape[1]), 0) - tops
    across = iota((width, lefts.shape[1]), 0) - lefts
    in_rows = jnp.where((down >= 0) & (down < STAMP), 1.0, 0.0).astype(jnp.bfloat16)
    in_cols = jnp.where((across >= 0) & (across < STAMP), 1.0, 0.0).astype(jnp.bfloat16)
    weights = dot(in_rows, in_cols, ((1,), (1,))) * inverse
    pieces = [p.astype(jnp.float32) for p in split3(science)]

    def constant_rows(group, row):
        block = jnp.zeros((SUB, width), jnp.float32)
        for extra in range(EXTRA):
            index = kernels + extra - group * SUB
            if 0 <= index < SUB:
                entry = (
                    jnp.ones((1, width), jnp.float32)
                    if extra == 0
                    else pieces[extra - 1][row : row + 1]
                )
                block = jnp.where(iota((SUB, width), 0) == index, entry, block)
        return block

    for copy in first:
        copy.wait_recv()
    for owner in range(n):
        tile[owner * share : (owner + 1) * share, :] = inbox[owner, 0:share, :]
    weight_total = inbox[0, share : 2 * share, :]
    for owner in range(1, n):
        weight_total = weight_total + inbox[owner, share : 2 * share, :]
    scale = jnp.sqrt(weight_total)

    columns = dot(tile[...].astype(jnp.bfloat16), col_bands[...]).astype(jnp.bfloat16)
    for group in range(groups):
        members = range(group * SUB, min((group + 1) * SUB, kernels))
        if len(members):
            block = jnp.concatenate([columns[:, k * width : (k + 1) * width] for k in members], 0)
            images = dot(row_bands[group, :, 0 : len(members) * height], block)
            images = images.astype(jnp.bfloat16).astype(jnp.float32)
        else:
            images = jnp.zeros((stacked, width), jnp.float32)
        for row in range(height):
            image = images[row * SUB : (row + 1) * SUB]
            if (group + 1) * SUB > kernels:
                image = image + constant_rows(group, row)
            design[row, group * SUB : (group + 1) * SUB, :] = image

    flat = jnp.concatenate([design[row] for row in range(height)], axis=1)
    flat_weights = jnp.concatenate([weights[row : row + 1] for row in range(height)], axis=1)
    gap = jnp.zeros((-flat.shape[0] % 16, flat.shape[1]), jnp.float32)
    flat = jnp.concatenate([flat, gap], axis=0)
    left = jnp.concatenate(split3(flat * flat_weights), axis=0)
    grams = dot(left, flat.astype(jnp.bfloat16), ((1,), (1,)))
    size = flat.shape[0]
    gram = grams[0:size] + grams[size : 2 * size] + grams[2 * size : 3 * size]
    gram = gram[0 : groups * SUB]
    unknowns = kernels + 1
    target = gram[:, unknowns : unknowns + 1]
    for extra in range(2, EXTRA):
        target = target + gram[:, kernels + extra : kernels + extra + 1]
    gram = jnp.where(iota(gram.shape, 1) == unknowns, target, gram)

    system = [gram[g * SUB : (g + 1) * SUB] for g in range(groups)]
    lanes_wide = system[0].shape[1]
    subs = iota((SUB, lanes_wide), 0)
    scales = [jnp.zeros((SUB, lanes_wide), jnp.float32) for _ in range(groups)]
    for k in range(unknowns):
        home, sub = divmod(k, SUB)
        row = jnp.broadcast_to(system[home][sub : sub + 1], (SUB, lanes_wide))
        pivot = 1.0 / jnp.broadcast_to(row[:, k : k + 1], (SUB, lanes_wide))
        scaled = row * pivot
        scales[home] = jnp.where(subs == sub, pivot, scales[home])
        for g in range(groups):
            factor = jnp.broadcast_to(system[g][:, k : k + 1], (SUB, lanes_wide))
            if g == home:
                factor = jnp.where(subs == sub, 0.0, factor)
            system[g] = system[g] - factor * scaled
    answers = [
        jnp.broadcast_to(system[g][:, unknowns : unknowns + 1] * scales[g][:, 0:1], (SUB, width))
        for g in range(groups)
    ]
    answer = jnp.concatenate(answers, axis=0)

    model = jnp.sum(design[...] * answer[None], axis=1)
    residual = science - model
    weighted = residual * inverse
    for owner in range(n):
        parts_out[owner] = weighted[owner * share : (owner + 1) * share]
    parts_in[me] = parts_out[me]
    second = copies(parts_out, parts_in, send_b, recv_b)
    for copy in second:
        copy.start()

    difference_ref[0] = residual / jnp.sqrt(variance)
    across = jnp.sum(
        jnp.where(iota(answer.shape, 0) == iota(answer.shape, 1), answer, 0.0), axis=0, keepdims=True
    )
    coefficients_ref[...] = across[:, 0:unknowns]

    for copy in second:
        copy.wait_recv()
    numerator = parts_in[0]
    for owner in range(1, n):
        numerator = numerator + parts_in[owner]
    detection_ref[...] = numerator / scale
    for copy in first + second:
        copy.wait_send()


def fused(n, template, science, variance, col_taps, row_taps, stamp_rows, stamp_cols):
    kernels = col_taps.shape[0]
    share, width = template.shape
    height = science.shape[1]
    groups = -(-(kernels + EXTRA) // SUB)
    stacked = SUB * height
    vmem = pl.BlockSpec(memory_space=pltpu.VMEM)
    return pl.pallas_call(
        functools.partial(fused_kernel, n),
        out_shape=(
            jax.ShapeDtypeStruct(science.shape, jnp.float32),
            jax.ShapeDtypeStruct((1, kernels + 1), jnp.float32),
            jax.ShapeDtypeStruct((share, width), jnp.float32),
        ),
        in_specs=[vmem] * 7,
        out_specs=(vmem,) * 3,
        scratch_shapes=[
            pltpu.VMEM((n, 2 * share, width), jnp.float32),
            pltpu.VMEM((n, 2 * share, width), jnp.float32),
            pltpu.VMEM((n, share, width), jnp.float32),
            pltpu.VMEM((n, share, width), jnp.float32),
            pltpu.VMEM((height, width), jnp.float32),
            pltpu.VMEM((width, kernels * width), jnp.bfloat16),
            pltpu.VMEM((groups, stacked, stacked), jnp.bfloat16),
            pltpu.VMEM((height, groups * SUB, width), jnp.float32),
            pltpu.SemaphoreType.DMA((n,)),
            pltpu.SemaphoreType.DMA((n,)),
            pltpu.SemaphoreType.DMA((n,)),
            pltpu.SemaphoreType.DMA((n,)),
        ],
        compiler_params=pltpu.CompilerParams(
            collective_id=0, has_side_effects=True, vmem_limit_bytes=32 * 2**20
        ),
    )(template, science, variance, col_taps, row_taps, stamp_rows, stamp_cols)


def per_device(axes, template, science, *rest):
    height, width = science.shape[1:]
    if axes["sky"] == 1 and width % 128 == 0 and SUB * height <= 2 * width:
        return fused(axes["visit"], template, science, *rest)
    return on_device(template, science, *rest)


def solution(mesh):
    in_specs = (
        P(("group", "visit"), "sky"),
        P(("group", "visit"), None, "sky"),
        P(("group", "visit"), None, "sky"),
        P(),
        P(),
        P(("group", "visit"), "sky", None),
        P(("group", "visit"), "sky", None),
    )
    out_specs = (
        P(("group", "visit"), None, "sky"),
        P(("group", "visit"), None),
        P(("group", "visit"), "sky"),
    )
    return jax.shard_map(
        functools.partial(per_device, dict(mesh.shape)), mesh=mesh, in_specs=in_specs, out_specs=out_specs, check_vma=False
    )
```

```python
import functools

import jax
import jax.numpy as jnp
from jax import lax
from jax.experimental import pallas as pl
from jax.experimental.pallas import tpu as pltpu
from jax.sharding import PartitionSpec as P

KBLK = 7
STAMP = 16


def with_halo(cells, sides, width):
    for axis, dim in sides:
        count = lax.axis_size(axis)
        ends = count - 1
        head = lax.slice_in_dim(cells, 0, width, axis=dim)
        tail = lax.slice_in_dim(cells, cells.shape[dim] - width, cells.shape[dim], axis=dim)
        cells = jnp.concatenate(
            [
                lax.ppermute(tail, axis, [(i, (i + 1) % count) for i in range(ends)]),
                cells,
                lax.ppermute(head, axis, [((i + 1) % count, i) for i in range(ends)]),
            ],
            axis=dim,
        )
    return cells


def tap_selectors(out_len, in_len, tap_count):
    offsets = (
        jnp.arange(in_len, dtype=jnp.int32)[None, :] - jnp.arange(out_len, dtype=jnp.int32)[:, None]
    )
    return (offsets[None, :, :] == jnp.arange(tap_count, dtype=jnp.int32)[:, None, None]).astype(
        jnp.float32
    )


def column_pass(padded, taps_block):
    tap_count = taps_block.shape[1]
    out_width = padded.shape[1] - tap_count + 1
    selectors = tap_selectors(out_width, padded.shape[1], tap_count)
    band_mats = jnp.einsum("kj,jci->kic", taps_block.astype(jnp.float32), selectors).astype(
        jnp.bfloat16
    )
    result = jnp.einsum("ri,kic->krc", padded, band_mats, preferred_element_type=jnp.float32)
    return result.astype(jnp.bfloat16)


def band_matrix(taps_block, out_len, in_len):
    tap_count = taps_block.shape[1]
    offsets = (
        jnp.arange(in_len, dtype=jnp.int32)[None, :] - jnp.arange(out_len, dtype=jnp.int32)[:, None]
    )
    taps_wide = taps_block.astype(jnp.float32)
    band = jnp.zeros((taps_block.shape[0], out_len, in_len), jnp.float32)
    for offset in range(tap_count):
        band = band + jnp.where(
            offsets[None, :, :] == offset, taps_wide[:, offset][:, None, None], 0.0
        )
    return band.astype(jnp.bfloat16)


def row_pass(columns, taps_block):
    tap_count = taps_block.shape[1]
    margin = (tap_count - 1) // 2
    height = columns.shape[1]
    stride = min(512, height)
    padded = jnp.pad(columns, ((0, 0), (margin, margin), (0, 0)))
    band = band_matrix(taps_block, stride, stride + 2 * margin)
    pieces = jnp.einsum("kti,kiw->ktw", band, padded, preferred_element_type=jnp.float32).astype(
        jnp.bfloat16
    )
    return pieces


def extract_stamps(block, row_starts, col_starts):

    def extract(row_start, col_start):
        return lax.dynamic_slice(
            block, (jnp.int32(0), row_start, col_start), (block.shape[0], STAMP, STAMP)
        )

    stamps = jax.vmap(extract)(row_starts, col_starts)
    return jnp.transpose(stamps, (1, 0, 2, 3)).reshape(block.shape[0], -1)


def extract_plane(plane, row_starts, col_starts):

    def extract(row_start, col_start):
        return lax.dynamic_slice(plane, (row_start, col_start), (STAMP, STAMP))

    return jax.vmap(extract)(row_starts, col_starts).reshape(-1)


def cholesky_solve(matrix, vector):
    factor = jnp.linalg.cholesky(matrix)
    middle = lax.linalg.triangular_solve(factor, vector[:, None], left_side=True, lower=True)
    answer = lax.linalg.triangular_solve(
        factor, middle, left_side=True, lower=True, transpose_a=True
    )
    return answer[:, 0]


def on_device(template, science, variance, col_taps, row_taps, stamp_rows, stamp_cols):
    tap_count = col_taps.shape[1]
    margin = (tap_count - 1) // 2
    kernels = col_taps.shape[0]
    blocks = kernels // KBLK
    science_map = science[0]
    variance_map = variance[0]
    inverse = 1.0 / variance_map
    gathered = lax.all_gather(template, "visit", axis=0, tiled=True)
    padded_tile = with_halo(gathered, (("sky", 1),), margin)
    image_list = []
    for block_index in range(blocks):
        image_list.append(
            row_pass(
                column_pass(padded_tile, col_taps[block_index * KBLK : (block_index + 1) * KBLK]),
                row_taps[block_index * KBLK : (block_index + 1) * KBLK],
            )
        )
    convolved = jnp.concatenate(image_list, axis=0)
    row_starts = stamp_rows[0, 0]
    col_starts = stamp_cols[0, 0]
    design_core = extract_stamps(convolved, row_starts, col_starts)
    design = jnp.concatenate(
        [design_core, jnp.ones((1, design_core.shape[1]), design_core.dtype)], axis=0
    ).astype(jnp.float32)
    weights = 1.0 / extract_plane(variance_map, row_starts, col_starts)
    values = extract_plane(science_map, row_starts, col_starts)
    partial_normal = jnp.dot(design * weights[None, :], design.T, precision=lax.Precision.HIGHEST)
    partial_target = jnp.dot(design, weights * values, precision=lax.Precision.HIGHEST)
    normal, target = lax.psum((partial_normal, partial_target), "sky")
    solution = cholesky_solve(normal, target)

    def model_step(block_index, total):
        images = lax.dynamic_slice_in_dim(convolved, block_index * KBLK, KBLK, 0).astype(
            jnp.float32
        )
        share = lax.dynamic_slice_in_dim(solution, block_index * KBLK, KBLK, 0)
        return total + jnp.tensordot(share, images, axes=1, precision=lax.Precision.HIGHEST)

    model_map = lax.fori_loop(0, blocks, model_step, jnp.zeros(science_map.shape, jnp.float32))
    residual = science_map - model_map - solution[kernels]
    difference = (residual / jnp.sqrt(variance_map))[None, :, :]
    weighted = residual / variance_map
    numerator, weight_total = (
        lax.psum_scatter(weighted, "visit", scatter_dimension=0, tiled=True),
        lax.psum_scatter(inverse, "visit", scatter_dimension=0, tiled=True),
    )
    detection = numerator / jnp.sqrt(weight_total)
    return (difference, solution[None, :], detection)


MESH = pl.DeviceIdType.MESH
SUB = 8
OPERANDS = 7
RESULTS = 3
VMEM_BYTES = 60 * 2**20
EXTRA = 4


def dot(a, b, contract=((1,), (0,))):
    return lax.dot_general(a, b, (contract, ((), ())), preferred_element_type=jnp.float32)


def split3(value):
    high = value.astype(jnp.bfloat16)
    rest = value - high.astype(jnp.float32)
    middle = rest.astype(jnp.bfloat16)
    low = (rest - middle.astype(jnp.float32)).astype(jnp.bfloat16)
    return high, middle, low


def iota(shape, dim):
    return lax.broadcasted_iota(jnp.int32, shape, dim)


def placed_taps(taps, lanes, sign):
    count = taps.shape[0]
    margin = (count - 1) // 2
    spot = sign * (iota((count, lanes), 0) - margin)
    spot = jnp.where(spot < 0, spot + lanes, spot)
    place = jnp.where(iota((count, lanes), 1) == spot, 1.0, 0.0).astype(jnp.bfloat16)
    return dot(taps, place, ((0,), (0,)))


def fused_kernel(
    n,
    *refs,
):
    operands, refs = refs[:OPERANDS], refs[OPERANDS:]
    results, refs = refs[:RESULTS], refs[RESULTS:]
    held, loaded, refs = refs[:OPERANDS], refs[OPERANDS], refs[OPERANDS + 1 :]
    ready, stored, refs = refs[:RESULTS], refs[RESULTS], refs[RESULTS + 1 :]
    stores = [
        pltpu.make_async_copy(here, result, stored.at[i])
        for i, (here, result) in enumerate(zip(ready, results))
    ]
    body(n, operands, held, loaded, stores, *ready, *refs)


def body(
    n,
    operands,
    held,
    loaded,
    stores,
    difference_ref,
    coefficients_ref,
    detection_ref,
    outbox,
    inbox,
    parts_out,
    parts_in,
    tile,
    col_bands,
    row_bands,
    design,
    send_a,
    recv_a,
    send_b,
    recv_b,
):
    template_ref, science_ref, variance_ref, col_taps_ref, row_taps_ref = held[:5]
    stamp_rows_ref, stamp_cols_ref = held[5:]
    me = lax.axis_index("visit")
    taps, kernels = col_taps_ref.shape
    margin = (taps - 1) // 2
    share, width = template_ref.shape
    height = science_ref.shape[1]
    groups = row_bands.shape[0]
    stacked = SUB * height

    def copies(source, target, send, recv):
        return [
            pltpu.make_async_remote_copy(
                src_ref=source.at[lax.rem(me + step, n)],
                dst_ref=target.at[me],
                send_sem=send.at[step],
                recv_sem=recv.at[step],
                device_id={"visit": lax.rem(me + step, n)},
                device_id_type=MESH,
            )
            for step in range(1, n)
        ]

    barrier = pltpu.get_barrier_semaphore()
    for step in range(1, n):
        pl.semaphore_signal(
            barrier, inc=1, device_id={"visit": lax.rem(me + step, n)}, device_id_type=MESH
        )

    fetches = [
        pltpu.make_async_copy(operand, here, loaded.at[i])
        for i, (operand, here) in enumerate(zip(operands, held))
    ]
    for fetch in fetches:
        fetch.start()
    for fetch in fetches:
        fetch.wait()

    science = science_ref[0]
    variance = variance_ref[0]
    inverse = 1.0 / variance
    own_rows = template_ref[...].astype(jnp.float32)
    for owner in range(n):
        outbox[owner, 0:share, :] = own_rows
        outbox[owner, share : 2 * share, :] = inverse[owner * share : (owner + 1) * share]
    inbox[me] = outbox[me]

    spread = placed_taps(row_taps_ref[...], width, 1)
    spread = jnp.concatenate(
        [spread, jnp.zeros((groups * SUB - kernels, width), jnp.float32)], axis=0
    )
    per_tile = width // height
    sub_of = iota((SUB, width), 0)
    for group in range(groups):
        source = spread[group * SUB : (group + 1) * SUB]
        base = source
        for slot in range(1, per_tile):
            base = jnp.where(sub_of % per_tile == slot, pltpu.roll(source, slot * height, 1), base)
        for row in range(0, height, 2):
            turned = [pltpu.roll(base, row + more, 1) for more in range(2)]
            for part in range(stacked // width):
                own = iota((SUB, width), 1) // height + part * per_tile == sub_of
                pair = [jnp.where(own, one, 0.0) for one in turned]
                row_bands[
                    group, row * SUB : (row + 2) * SUB, part * width : (part + 1) * width
                ] = jnp.concatenate(pair, axis=0).astype(jnp.bfloat16)

    pl.semaphore_wait(barrier, n - 1)
    first = copies(outbox, inbox, send_a, recv_a)
    for copy in first:
        copy.start()

    lanes = placed_taps(col_taps_ref[...], width, -1)
    near = jnp.abs(iota((width, width), 0) - iota((width, width), 1)) <= margin
    for k in range(kernels):
        base = pltpu.roll(
            jnp.broadcast_to(lanes[k : k + 1], (width, width)), 0, 1, stride=1, stride_axis=0
        )
        col_bands[:, k * width : (k + 1) * width] = jnp.where(near, base, 0.0).astype(jnp.bfloat16)

    tops = stamp_rows_ref[0]
    lefts = stamp_cols_ref[0]
    down = iota((height, tops.shape[1]), 0) - tops
    across = iota((width, lefts.shape[1]), 0) - lefts
    in_rows = jnp.where((down >= 0) & (down < STAMP), 1.0, 0.0).astype(jnp.bfloat16)
    in_cols = jnp.where((across >= 0) & (across < STAMP), 1.0, 0.0).astype(jnp.bfloat16)
    weights = dot(in_rows, in_cols, ((1,), (1,))) * inverse
    pieces = [p.astype(jnp.float32) for p in split3(science)]

    def constant_rows(group, row):
        block = jnp.zeros((SUB, width), jnp.float32)
        for extra in range(EXTRA):
            index = kernels + extra - group * SUB
            if 0 <= index < SUB:
                entry = (
                    jnp.ones((1, width), jnp.float32)
                    if extra == 0
                    else pieces[extra - 1][row : row + 1]
                )
                block = jnp.where(iota((SUB, width), 0) == index, entry, block)
        return block

    for copy in first:
        copy.wait_recv()
    for owner in range(n):
        tile[owner * share : (owner + 1) * share, :] = inbox[owner, 0:share, :]
    weight_total = inbox[0, share : 2 * share, :]
    for owner in range(1, n):
        weight_total = weight_total + inbox[owner, share : 2 * share, :]
    scale = jnp.sqrt(weight_total)

    columns = dot(tile[...].astype(jnp.bfloat16), col_bands[...]).astype(jnp.bfloat16)
    for group in range(groups):
        members = range(group * SUB, min((group + 1) * SUB, kernels))
        if len(members):
            block = jnp.concatenate([columns[:, k * width : (k + 1) * width] for k in members], 0)
            images = dot(row_bands[group, :, 0 : len(members) * height], block)
            images = images.astype(jnp.bfloat16).astype(jnp.float32)
        else:
            images = jnp.zeros((stacked, width), jnp.float32)
        for row in range(height):
            image = images[row * SUB : (row + 1) * SUB]
            if (group + 1) * SUB > kernels:
                image = image + constant_rows(group, row)
            design[row, group * SUB : (group + 1) * SUB, :] = image

    flat = jnp.concatenate([design[row] for row in range(height)], axis=1)
    flat_weights = jnp.concatenate([weights[row : row + 1] for row in range(height)], axis=1)
    gap = jnp.zeros((-flat.shape[0] % 16, flat.shape[1]), jnp.float32)
    flat = jnp.concatenate([flat, gap], axis=0)
    left = jnp.concatenate(split3(flat * flat_weights), axis=0)
    grams = dot(left, flat.astype(jnp.bfloat16), ((1,), (1,)))
    size = flat.shape[0]
    gram = grams[0:size] + grams[size : 2 * size] + grams[2 * size : 3 * size]
    gram = gram[0 : groups * SUB]
    unknowns = kernels + 1
    target = gram[:, unknowns : unknowns + 1]
    for extra in range(2, EXTRA):
        target = target + gram[:, kernels + extra : kernels + extra + 1]
    gram = jnp.where(iota(gram.shape, 1) == unknowns, target, gram)

    system = [gram[g * SUB : (g + 1) * SUB] for g in range(groups)]
    shape = system[0].shape
    subs = iota(shape, 0)
    for home in range(groups):
        begin = home * SUB
        size = min(SUB, unknowns - begin)
        if size <= 0:
            break
        factors = [
            [jnp.broadcast_to(part[:, begin + s : begin + s + 1], shape) for s in range(size)]
            for part in system
        ]
        rows = [jnp.broadcast_to(system[home][s : s + 1], shape) for s in range(size)]
        pivots = [
            [jnp.broadcast_to(factors[home][s][t : t + 1], shape) for s in range(size)]
            for t in range(size)
        ]
        for s in range(size):
            scale_by = 1.0 / pivots[s][s]
            for u in range(s + 1, size):
                pivots[s][u] = pivots[s][u] * scale_by
            rows[s] = rows[s] * scale_by
            for t in range(size):
                if t == s:
                    continue
                by = pivots[t][s]
                for u in range(s + 1, size):
                    pivots[t][u] = pivots[t][u] - by * pivots[s][u]
                rows[t] = rows[t] - by * rows[s]
        for g in range(groups):
            if g == home:
                for s in range(size):
                    system[g] = jnp.where(subs == s, rows[s], system[g])
                continue
            change = factors[g][0] * rows[0]
            for s in range(1, size):
                change = change + factors[g][s] * rows[s]
            system[g] = system[g] - change
    answers = [
        jnp.where(
            iota((SUB, width), 0) + g * SUB < unknowns,
            jnp.broadcast_to(system[g][:, unknowns : unknowns + 1], (SUB, width)),
            0.0,
        )
        for g in range(groups)
    ]
    answer = jnp.concatenate(answers, axis=0)

    model = jnp.sum(design[...] * answer[None], axis=1)
    residual = science - model
    weighted = residual * inverse
    for owner in range(n):
        parts_out[owner] = weighted[owner * share : (owner + 1) * share]
    parts_in[me] = parts_out[me]
    second = copies(parts_out, parts_in, send_b, recv_b)
    for copy in second:
        copy.start()

    difference_ref[0] = residual / jnp.sqrt(variance)
    across = jnp.sum(
        jnp.where(iota(answer.shape, 0) == iota(answer.shape, 1), answer, 0.0), axis=0, keepdims=True
    )
    coefficients_ref[...] = across[:, 0:unknowns]
    for store in stores[:-1]:
        store.start()

    for copy in second:
        copy.wait_recv()
    numerator = parts_in[0]
    for owner in range(1, n):
        numerator = numerator + parts_in[owner]
    detection_ref[...] = numerator / scale
    stores[-1].start()
    for copy in first + second:
        copy.wait_send()
    for store in stores:
        store.wait()


def hand_over(*refs):
    done = refs[-1]
    moves = [
        pltpu.make_async_copy(refs[i], refs[RESULTS + i], done.at[i]) for i in range(RESULTS)
    ]
    for move in moves:
        move.start()
    for move in moves:
        move.wait()


def fused(n, template, science, variance, col_taps, row_taps, stamp_rows, stamp_cols):
    kernels = col_taps.shape[0]
    share, width = template.shape
    height = science.shape[1]
    groups = -(-(kernels + EXTRA) // SUB)
    stacked = SUB * height
    hbm = pl.BlockSpec(memory_space=pltpu.HBM)
    operands = (template, science, variance, col_taps.T, row_taps.T, stamp_rows, stamp_cols)
    shapes = (
        jax.ShapeDtypeStruct(science.shape, jnp.float32),
        jax.ShapeDtypeStruct((1, kernels + 1), jnp.float32),
        jax.ShapeDtypeStruct((share, width), jnp.float32),
    )
    results = pl.pallas_call(
        functools.partial(fused_kernel, n),
        out_shape=shapes,
        in_specs=[hbm] * OPERANDS,
        out_specs=(hbm,) * RESULTS,
        scratch_shapes=[pltpu.VMEM(operand.shape, operand.dtype) for operand in operands]
        + [
            pltpu.SemaphoreType.DMA((OPERANDS,)),
        ]
        + [pltpu.VMEM(shape.shape, shape.dtype) for shape in shapes]
        + [
            pltpu.SemaphoreType.DMA((RESULTS,)),
            pltpu.VMEM((n, 2 * share, width), jnp.float32),
            pltpu.VMEM((n, 2 * share, width), jnp.float32),
            pltpu.VMEM((n, share, width), jnp.float32),
            pltpu.VMEM((n, share, width), jnp.float32),
            pltpu.VMEM((height, width), jnp.float32),
            pltpu.VMEM((width, kernels * width), jnp.bfloat16),
            pltpu.VMEM((groups, stacked, stacked), jnp.bfloat16),
            pltpu.VMEM((height, groups * SUB, width), jnp.float32),
            pltpu.SemaphoreType.DMA((n,)),
            pltpu.SemaphoreType.DMA((n,)),
            pltpu.SemaphoreType.DMA((n,)),
            pltpu.SemaphoreType.DMA((n,)),
        ],
        compiler_params=pltpu.CompilerParams(
            collective_id=0, has_side_effects=True, vmem_limit_bytes=VMEM_BYTES
        ),
    )(*operands)
    return pl.pallas_call(
        hand_over,
        out_shape=shapes,
        in_specs=[hbm] * RESULTS,
        out_specs=(hbm,) * RESULTS,
        scratch_shapes=[pltpu.SemaphoreType.DMA((RESULTS,))],
        compiler_params=pltpu.CompilerParams(vmem_limit_bytes=VMEM_BYTES),
    )(*results)


def per_device(axes, template, science, *rest):
    height, width = science.shape[1:]
    if axes["sky"] == 1 and width % 128 == 0 and SUB * height == 2 * width:
        return fused(axes["visit"], template, science, *rest)
    return on_device(template, science, *rest)


def solution(mesh):
    in_specs = (
        P(("group", "visit"), "sky"),
        P(("group", "visit"), None, "sky"),
        P(("group", "visit"), None, "sky"),
        P(),
        P(),
        P(("group", "visit"), "sky", None),
        P(("group", "visit"), "sky", None),
    )
    out_specs = (
        P(("group", "visit"), None, "sky"),
        P(("group", "visit"), None),
        P(("group", "visit"), "sky"),
    )
    return jax.shard_map(
        functools.partial(per_device, dict(mesh.shape)), mesh=mesh, in_specs=in_specs, out_specs=out_specs, check_vma=False
    )
```

```python
import functools

import jax
import jax.numpy as jnp
from jax import lax
from jax.experimental import pallas as pl
from jax.experimental.pallas import tpu as pltpu
from jax.sharding import PartitionSpec as P

KBLK = 7
STAMP = 16


def with_halo(cells, sides, width):
    for axis, dim in sides:
        count = lax.axis_size(axis)
        ends = count - 1
        head = lax.slice_in_dim(cells, 0, width, axis=dim)
        tail = lax.slice_in_dim(cells, cells.shape[dim] - width, cells.shape[dim], axis=dim)
        cells = jnp.concatenate(
            [
                lax.ppermute(tail, axis, [(i, (i + 1) % count) for i in range(ends)]),
                cells,
                lax.ppermute(head, axis, [((i + 1) % count, i) for i in range(ends)]),
            ],
            axis=dim,
        )
    return cells


def tap_selectors(out_len, in_len, tap_count):
    offsets = (
        jnp.arange(in_len, dtype=jnp.int32)[None, :] - jnp.arange(out_len, dtype=jnp.int32)[:, None]
    )
    return (offsets[None, :, :] == jnp.arange(tap_count, dtype=jnp.int32)[:, None, None]).astype(
        jnp.float32
    )


def column_pass(padded, taps_block):
    tap_count = taps_block.shape[1]
    out_width = padded.shape[1] - tap_count + 1
    selectors = tap_selectors(out_width, padded.shape[1], tap_count)
    band_mats = jnp.einsum("kj,jci->kic", taps_block.astype(jnp.float32), selectors).astype(
        jnp.bfloat16
    )
    result = jnp.einsum("ri,kic->krc", padded, band_mats, preferred_element_type=jnp.float32)
    return result.astype(jnp.bfloat16)


def band_matrix(taps_block, out_len, in_len):
    tap_count = taps_block.shape[1]
    offsets = (
        jnp.arange(in_len, dtype=jnp.int32)[None, :] - jnp.arange(out_len, dtype=jnp.int32)[:, None]
    )
    taps_wide = taps_block.astype(jnp.float32)
    band = jnp.zeros((taps_block.shape[0], out_len, in_len), jnp.float32)
    for offset in range(tap_count):
        band = band + jnp.where(
            offsets[None, :, :] == offset, taps_wide[:, offset][:, None, None], 0.0
        )
    return band.astype(jnp.bfloat16)


def row_pass(columns, taps_block):
    tap_count = taps_block.shape[1]
    margin = (tap_count - 1) // 2
    height = columns.shape[1]
    stride = min(512, height)
    padded = jnp.pad(columns, ((0, 0), (margin, margin), (0, 0)))
    band = band_matrix(taps_block, stride, stride + 2 * margin)
    pieces = jnp.einsum("kti,kiw->ktw", band, padded, preferred_element_type=jnp.float32).astype(
        jnp.bfloat16
    )
    return pieces


def extract_stamps(block, row_starts, col_starts):

    def extract(row_start, col_start):
        return lax.dynamic_slice(
            block, (jnp.int32(0), row_start, col_start), (block.shape[0], STAMP, STAMP)
        )

    stamps = jax.vmap(extract)(row_starts, col_starts)
    return jnp.transpose(stamps, (1, 0, 2, 3)).reshape(block.shape[0], -1)


def extract_plane(plane, row_starts, col_starts):

    def extract(row_start, col_start):
        return lax.dynamic_slice(plane, (row_start, col_start), (STAMP, STAMP))

    return jax.vmap(extract)(row_starts, col_starts).reshape(-1)


def cholesky_solve(matrix, vector):
    factor = jnp.linalg.cholesky(matrix)
    middle = lax.linalg.triangular_solve(factor, vector[:, None], left_side=True, lower=True)
    answer = lax.linalg.triangular_solve(
        factor, middle, left_side=True, lower=True, transpose_a=True
    )
    return answer[:, 0]


def on_device(template, science, variance, col_taps, row_taps, stamp_rows, stamp_cols):
    tap_count = col_taps.shape[1]
    margin = (tap_count - 1) // 2
    kernels = col_taps.shape[0]
    blocks = kernels // KBLK
    science_map = science[0]
    variance_map = variance[0]
    inverse = 1.0 / variance_map
    gathered = lax.all_gather(template, "visit", axis=0, tiled=True)
    padded_tile = with_halo(gathered, (("sky", 1),), margin)
    image_list = []
    for block_index in range(blocks):
        image_list.append(
            row_pass(
                column_pass(padded_tile, col_taps[block_index * KBLK : (block_index + 1) * KBLK]),
                row_taps[block_index * KBLK : (block_index + 1) * KBLK],
            )
        )
    convolved = jnp.concatenate(image_list, axis=0)
    row_starts = stamp_rows[0, 0]
    col_starts = stamp_cols[0, 0]
    design_core = extract_stamps(convolved, row_starts, col_starts)
    design = jnp.concatenate(
        [design_core, jnp.ones((1, design_core.shape[1]), design_core.dtype)], axis=0
    ).astype(jnp.float32)
    weights = 1.0 / extract_plane(variance_map, row_starts, col_starts)
    values = extract_plane(science_map, row_starts, col_starts)
    partial_normal = jnp.dot(design * weights[None, :], design.T, precision=lax.Precision.HIGHEST)
    partial_target = jnp.dot(design, weights * values, precision=lax.Precision.HIGHEST)
    normal, target = lax.psum((partial_normal, partial_target), "sky")
    solution = cholesky_solve(normal, target)

    def model_step(block_index, total):
        images = lax.dynamic_slice_in_dim(convolved, block_index * KBLK, KBLK, 0).astype(
            jnp.float32
        )
        share = lax.dynamic_slice_in_dim(solution, block_index * KBLK, KBLK, 0)
        return total + jnp.tensordot(share, images, axes=1, precision=lax.Precision.HIGHEST)

    model_map = lax.fori_loop(0, blocks, model_step, jnp.zeros(science_map.shape, jnp.float32))
    residual = science_map - model_map - solution[kernels]
    difference = (residual / jnp.sqrt(variance_map))[None, :, :]
    weighted = residual / variance_map
    numerator, weight_total = (
        lax.psum_scatter(weighted, "visit", scatter_dimension=0, tiled=True),
        lax.psum_scatter(inverse, "visit", scatter_dimension=0, tiled=True),
    )
    detection = numerator / jnp.sqrt(weight_total)
    return (difference, solution[None, :], detection)


MESH = pl.DeviceIdType.MESH
SUB = 8
OPERANDS = 7
RESULTS = 3
VMEM_BYTES = 60 * 2**20
EXTRA = 4


def dot(a, b, contract=((1,), (0,))):
    return lax.dot_general(a, b, (contract, ((), ())), preferred_element_type=jnp.float32)


def split3(value):
    high = value.astype(jnp.bfloat16)
    rest = value - high.astype(jnp.float32)
    middle = rest.astype(jnp.bfloat16)
    low = (rest - middle.astype(jnp.float32)).astype(jnp.bfloat16)
    return high, middle, low


def iota(shape, dim):
    return lax.broadcasted_iota(jnp.int32, shape, dim)


def placed_taps(taps, lanes, spot, block):
    count = taps.shape[0]
    here = iota((count, lanes), 1) // block == spot(iota((count, lanes), 0))
    return dot(taps, jnp.where(here, 1.0, 0.0).astype(jnp.bfloat16), ((0,), (0,)))


def padded_rows(value, rows):
    gap = jnp.zeros((rows - value.shape[0], value.shape[1]), value.dtype)
    return jnp.concatenate([value, gap], axis=0)


def reciprocal(value):
    guess = pl.reciprocal(value, approx=True)
    guess = guess * (2.0 - value * guess)
    return guess * (2.0 - value * guess)


def fused_kernel(
    n,
    *refs,
):
    operands, refs = refs[:OPERANDS], refs[OPERANDS:]
    results, refs = refs[:RESULTS], refs[RESULTS:]
    held, loaded, refs = refs[:OPERANDS], refs[OPERANDS], refs[OPERANDS + 1 :]
    ready, stored, refs = refs[:RESULTS], refs[RESULTS], refs[RESULTS + 1 :]
    stores = [
        pltpu.make_async_copy(here, result, stored.at[i])
        for i, (here, result) in enumerate(zip(ready, results))
    ]
    body(n, operands, held, loaded, stores, *ready, *refs)


def body(
    n,
    operands,
    held,
    loaded,
    stores,
    difference_ref,
    coefficients_ref,
    detection_ref,
    outbox,
    inbox,
    parts_out,
    parts_in,
    tile,
    row_bands,
    design,
    send_a,
    recv_a,
    send_b,
    recv_b,
):
    template_ref, science_ref, variance_ref, col_taps_ref, row_taps_ref = held[:5]
    stamp_rows_ref, stamp_cols_ref = held[5:]
    me = lax.axis_index("visit")
    taps, kernels = col_taps_ref.shape
    margin = (taps - 1) // 2
    share, width = template_ref.shape
    height = science_ref.shape[1]
    groups = row_bands.shape[0]
    stacked = SUB * height

    def copies(source, target, send, recv):
        return [
            pltpu.make_async_remote_copy(
                src_ref=source.at[lax.rem(me + step, n)],
                dst_ref=target.at[me],
                send_sem=send.at[step],
                recv_sem=recv.at[step],
                device_id={"visit": lax.rem(me + step, n)},
                device_id_type=MESH,
            )
            for step in range(1, n)
        ]

    barrier = pltpu.get_barrier_semaphore()
    for step in range(1, n):
        pl.semaphore_signal(
            barrier, inc=1, device_id={"visit": lax.rem(me + step, n)}, device_id_type=MESH
        )

    fetches = [
        pltpu.make_async_copy(operand, here, loaded.at[i])
        for i, (operand, here) in enumerate(zip(operands, held))
    ]
    for fetch in fetches:
        fetch.start()
    for fetch in fetches[:3]:
        fetch.wait()

    science = science_ref[0]
    variance = variance_ref[0]
    inverse = 1.0 / variance
    own_rows = template_ref[...].astype(jnp.float32)
    for owner in range(n):
        outbox[owner, 0:share, :] = own_rows
        outbox[owner, share : 2 * share, :] = inverse[owner * share : (owner + 1) * share]
    inbox[me] = outbox[me]

    for fetch in fetches[3:]:
        fetch.wait()

    spread = placed_taps(
        row_taps_ref[...],
        stacked,
        lambda j: jnp.where(j < margin, j - margin + height, j - margin),
        SUB,
    )
    spread = padded_rows(spread, groups * SUB)
    own = iota((SUB, stacked), 1) % SUB == iota((SUB, stacked), 0)
    lane_row = iota((SUB, stacked), 1) // SUB
    for group in range(groups):
        base = jnp.where(own, spread[group * SUB : (group + 1) * SUB], 0.0)
        for row in range(0, height, 2):
            pair = [
                jnp.where(
                    jnp.abs(lane_row - (row + more)) <= margin,
                    pltpu.roll(base, SUB * (row + more), 1) if row + more else base,
                    0.0,
                )
                for more in range(2)
            ]
            row_bands[group, row * SUB : (row + 2) * SUB, :] = jnp.concatenate(
                pair, axis=0
            ).astype(jnp.bfloat16)

    pl.semaphore_wait(barrier, n - 1)
    first = copies(outbox, inbox, send_a, recv_a)
    for copy in first:
        copy.start()

    depth = -(-taps // 16) * 16
    col_taps = placed_taps(col_taps_ref[...], depth, lambda j: taps - 1 - j, 1)
    col_taps = padded_rows(col_taps, -(-groups * SUB // 16) * 16).astype(jnp.bfloat16)
    source_col = iota((depth, width), 1) + margin - iota((depth, width), 0)
    inside = (source_col >= 0) & (source_col < width)

    tops = stamp_rows_ref[0]
    lefts = stamp_cols_ref[0]
    down = iota((height, tops.shape[1]), 0) - tops
    across = iota((width, lefts.shape[1]), 0) - lefts
    in_rows = jnp.where((down >= 0) & (down < STAMP), 1.0, 0.0).astype(jnp.bfloat16)
    in_cols = jnp.where((across >= 0) & (across < STAMP), 1.0, 0.0).astype(jnp.bfloat16)
    weights = dot(in_rows, in_cols, ((1,), (1,))) * inverse
    pieces = [p.astype(jnp.float32) for p in split3(science)]

    def constant_rows(group, row):
        block = jnp.zeros((SUB, width), jnp.float32)
        for extra in range(EXTRA):
            index = kernels + extra - group * SUB
            if 0 <= index < SUB:
                entry = (
                    jnp.ones((1, width), jnp.float32)
                    if extra == 0
                    else pieces[extra - 1][row : row + 1]
                )
                block = jnp.where(iota((SUB, width), 0) == index, entry, block)
        return block

    for copy in first:
        copy.wait_recv()
    for owner in range(n):
        tile[owner * share : (owner + 1) * share, :] = inbox[owner, 0:share, :]
    weight_total = inbox[0, share : 2 * share, :]
    for owner in range(1, n):
        weight_total = weight_total + inbox[owner, share : 2 * share, :]
    scale = jnp.sqrt(weight_total)

    shifted = [
        jnp.where(
            inside,
            pltpu.roll(
                jnp.broadcast_to(tile[row : row + 1, :], (depth, width)),
                width - margin,
                1,
                stride=1,
                stride_axis=0,
            ),
            0.0,
        ).astype(jnp.bfloat16)
        for row in range(height)
    ]
    columns = dot(col_taps, jnp.concatenate(shifted, axis=1))
    for group in range(groups):
        block = jnp.concatenate(
            [
                columns[group * SUB : (group + 1) * SUB, row * width : (row + 1) * width]
                for row in range(height)
            ],
            axis=0,
        ).astype(jnp.bfloat16)
        images = dot(row_bands[group], block).astype(jnp.bfloat16).astype(jnp.float32)
        for row in range(height):
            image = images[row * SUB : (row + 1) * SUB]
            if (group + 1) * SUB > kernels:
                image = image + constant_rows(group, row)
            design[row, group * SUB : (group + 1) * SUB, :] = image

    flat = jnp.concatenate([design[row] for row in range(height)], axis=1)
    flat_weights = jnp.concatenate([weights[row : row + 1] for row in range(height)], axis=1)
    gap = jnp.zeros((-flat.shape[0] % 16, flat.shape[1]), jnp.float32)
    flat = jnp.concatenate([flat, gap], axis=0)
    left = jnp.concatenate(split3(flat * flat_weights), axis=0)
    grams = dot(left, flat.astype(jnp.bfloat16), ((1,), (1,)))
    size = flat.shape[0]
    gram = grams[0:size] + grams[size : 2 * size] + grams[2 * size : 3 * size]
    gram = gram[0 : groups * SUB]
    unknowns = kernels + 1
    target = gram[:, unknowns : unknowns + 1]
    for extra in range(2, EXTRA):
        target = target + gram[:, kernels + extra : kernels + extra + 1]
    gram = jnp.where(iota(gram.shape, 1) == unknowns, target, gram)

    system = [gram[g * SUB : (g + 1) * SUB] for g in range(groups)]
    shape = system[0].shape
    subs = iota(shape, 0)
    for home in range(groups):
        begin = home * SUB
        size = min(SUB, unknowns - begin)
        if size <= 0:
            break
        factors = [
            [jnp.broadcast_to(part[:, begin + s : begin + s + 1], shape) for s in range(size)]
            for part in system
        ]
        rows = [jnp.broadcast_to(system[home][s : s + 1], shape) for s in range(size)]
        pivots = [
            [jnp.broadcast_to(factors[home][s][t : t + 1], shape) for s in range(size)]
            for t in range(size)
        ]
        for s in range(size):
            scale_by = reciprocal(pivots[s][s])
            for u in range(s + 1, size):
                pivots[s][u] = pivots[s][u] * scale_by
            rows[s] = rows[s] * scale_by
            for t in range(size):
                if t == s:
                    continue
                by = pivots[t][s]
                for u in range(s + 1, size):
                    pivots[t][u] = pivots[t][u] - by * pivots[s][u]
                rows[t] = rows[t] - by * rows[s]
        for g in range(groups):
            if g == home:
                for s in range(size):
                    system[g] = jnp.where(subs == s, rows[s], system[g])
                continue
            change = factors[g][0] * rows[0]
            for s in range(1, size):
                change = change + factors[g][s] * rows[s]
            system[g] = system[g] - change
    answers = [
        jnp.where(
            iota((SUB, width), 0) + g * SUB < unknowns,
            jnp.broadcast_to(system[g][:, unknowns : unknowns + 1], (SUB, width)),
            0.0,
        )
        for g in range(groups)
    ]
    answer = jnp.concatenate(answers, axis=0)

    model = jnp.sum(design[...] * answer[None], axis=1)
    residual = science - model
    weighted = residual * inverse
    for owner in range(n):
        parts_out[owner] = weighted[owner * share : (owner + 1) * share]
    parts_in[me] = parts_out[me]
    second = copies(parts_out, parts_in, send_b, recv_b)
    for copy in second:
        copy.start()

    difference_ref[0] = residual / jnp.sqrt(variance)
    across = jnp.sum(
        jnp.where(iota(answer.shape, 0) == iota(answer.shape, 1), answer, 0.0), axis=0, keepdims=True
    )
    coefficients_ref[...] = across[:, 0:unknowns]
    for store in stores[:-1]:
        store.start()

    for copy in second:
        copy.wait_recv()
    numerator = parts_in[0]
    for owner in range(1, n):
        numerator = numerator + parts_in[owner]
    detection_ref[...] = numerator / scale
    stores[-1].start()
    for copy in first + second:
        copy.wait_send()
    for store in stores:
        store.wait()


def hand_over(*refs):
    done = refs[-1]
    moves = [
        pltpu.make_async_copy(refs[i], refs[RESULTS + i], done.at[i]) for i in range(RESULTS)
    ]
    for move in moves:
        move.start()
    for move in moves:
        move.wait()


def fused(n, template, science, variance, col_taps, row_taps, stamp_rows, stamp_cols):
    kernels = col_taps.shape[0]
    share, width = template.shape
    height = science.shape[1]
    groups = -(-(kernels + EXTRA) // SUB)
    stacked = SUB * height
    hbm = pl.BlockSpec(memory_space=pltpu.HBM)
    operands = (template, science, variance, col_taps.T, row_taps.T, stamp_rows, stamp_cols)
    shapes = (
        jax.ShapeDtypeStruct(science.shape, jnp.float32),
        jax.ShapeDtypeStruct((1, kernels + 1), jnp.float32),
        jax.ShapeDtypeStruct((share, width), jnp.float32),
    )
    results = pl.pallas_call(
        functools.partial(fused_kernel, n),
        out_shape=shapes,
        in_specs=[hbm] * OPERANDS,
        out_specs=(hbm,) * RESULTS,
        scratch_shapes=[pltpu.VMEM(operand.shape, operand.dtype) for operand in operands]
        + [
            pltpu.SemaphoreType.DMA((OPERANDS,)),
        ]
        + [pltpu.VMEM(shape.shape, shape.dtype) for shape in shapes]
        + [
            pltpu.SemaphoreType.DMA((RESULTS,)),
            pltpu.VMEM((n, 2 * share, width), jnp.float32),
            pltpu.VMEM((n, 2 * share, width), jnp.float32),
            pltpu.VMEM((n, share, width), jnp.float32),
            pltpu.VMEM((n, share, width), jnp.float32),
            pltpu.VMEM((height, width), jnp.float32),
            pltpu.VMEM((groups, stacked, stacked), jnp.bfloat16),
            pltpu.VMEM((height, groups * SUB, width), jnp.float32),
            pltpu.SemaphoreType.DMA((n,)),
            pltpu.SemaphoreType.DMA((n,)),
            pltpu.SemaphoreType.DMA((n,)),
            pltpu.SemaphoreType.DMA((n,)),
        ],
        compiler_params=pltpu.CompilerParams(
            collective_id=0, has_side_effects=True, vmem_limit_bytes=VMEM_BYTES
        ),
    )(*operands)
    return pl.pallas_call(
        hand_over,
        out_shape=shapes,
        in_specs=[hbm] * RESULTS,
        out_specs=(hbm,) * RESULTS,
        scratch_shapes=[pltpu.SemaphoreType.DMA((RESULTS,))],
        compiler_params=pltpu.CompilerParams(vmem_limit_bytes=VMEM_BYTES),
    )(*results)


def per_device(axes, template, science, *rest):
    height, width = science.shape[1:]
    if axes["sky"] == 1 and width % 128 == 0 and SUB * height == 2 * width and rest[1].shape[1] <= height:
        return fused(axes["visit"], template, science, *rest)
    return on_device(template, science, *rest)


def solution(mesh):
    in_specs = (
        P(("group", "visit"), "sky"),
        P(("group", "visit"), None, "sky"),
        P(("group", "visit"), None, "sky"),
        P(),
        P(),
        P(("group", "visit"), "sky", None),
        P(("group", "visit"), "sky", None),
    )
    out_specs = (
        P(("group", "visit"), None, "sky"),
        P(("group", "visit"), None),
        P(("group", "visit"), "sky"),
    )
    return jax.shard_map(
        functools.partial(per_device, dict(mesh.shape)), mesh=mesh, in_specs=in_specs, out_specs=out_specs, check_vma=False
    )
```

```python
import functools

import jax
import jax.numpy as jnp
from jax import lax
from jax.experimental import pallas as pl
from jax.experimental.pallas import tpu as pltpu
from jax.sharding import PartitionSpec as P

KBLK = 7
STAMP = 16


def with_halo(cells, sides, width):
    for axis, dim in sides:
        count = lax.axis_size(axis)
        ends = count - 1
        head = lax.slice_in_dim(cells, 0, width, axis=dim)
        tail = lax.slice_in_dim(cells, cells.shape[dim] - width, cells.shape[dim], axis=dim)
        cells = jnp.concatenate(
            [
                lax.ppermute(tail, axis, [(i, (i + 1) % count) for i in range(ends)]),
                cells,
                lax.ppermute(head, axis, [((i + 1) % count, i) for i in range(ends)]),
            ],
            axis=dim,
        )
    return cells


def tap_selectors(out_len, in_len, tap_count):
    offsets = (
        jnp.arange(in_len, dtype=jnp.int32)[None, :] - jnp.arange(out_len, dtype=jnp.int32)[:, None]
    )
    return (offsets[None, :, :] == jnp.arange(tap_count, dtype=jnp.int32)[:, None, None]).astype(
        jnp.float32
    )


def column_pass(padded, taps_block):
    tap_count = taps_block.shape[1]
    out_width = padded.shape[1] - tap_count + 1
    selectors = tap_selectors(out_width, padded.shape[1], tap_count)
    band_mats = jnp.einsum("kj,jci->kic", taps_block.astype(jnp.float32), selectors).astype(
        jnp.bfloat16
    )
    result = jnp.einsum("ri,kic->krc", padded, band_mats, preferred_element_type=jnp.float32)
    return result.astype(jnp.bfloat16)


def band_matrix(taps_block, out_len, in_len):
    tap_count = taps_block.shape[1]
    offsets = (
        jnp.arange(in_len, dtype=jnp.int32)[None, :] - jnp.arange(out_len, dtype=jnp.int32)[:, None]
    )
    taps_wide = taps_block.astype(jnp.float32)
    band = jnp.zeros((taps_block.shape[0], out_len, in_len), jnp.float32)
    for offset in range(tap_count):
        band = band + jnp.where(
            offsets[None, :, :] == offset, taps_wide[:, offset][:, None, None], 0.0
        )
    return band.astype(jnp.bfloat16)


def row_pass(columns, taps_block):
    tap_count = taps_block.shape[1]
    margin = (tap_count - 1) // 2
    height = columns.shape[1]
    stride = min(512, height)
    padded = jnp.pad(columns, ((0, 0), (margin, margin), (0, 0)))
    band = band_matrix(taps_block, stride, stride + 2 * margin)
    pieces = jnp.einsum("kti,kiw->ktw", band, padded, preferred_element_type=jnp.float32).astype(
        jnp.bfloat16
    )
    return pieces


def extract_stamps(block, row_starts, col_starts):

    def extract(row_start, col_start):
        return lax.dynamic_slice(
            block, (jnp.int32(0), row_start, col_start), (block.shape[0], STAMP, STAMP)
        )

    stamps = jax.vmap(extract)(row_starts, col_starts)
    return jnp.transpose(stamps, (1, 0, 2, 3)).reshape(block.shape[0], -1)


def extract_plane(plane, row_starts, col_starts):

    def extract(row_start, col_start):
        return lax.dynamic_slice(plane, (row_start, col_start), (STAMP, STAMP))

    return jax.vmap(extract)(row_starts, col_starts).reshape(-1)


def cholesky_solve(matrix, vector):
    factor = jnp.linalg.cholesky(matrix)
    middle = lax.linalg.triangular_solve(factor, vector[:, None], left_side=True, lower=True)
    answer = lax.linalg.triangular_solve(
        factor, middle, left_side=True, lower=True, transpose_a=True
    )
    return answer[:, 0]


def on_device(template, science, variance, col_taps, row_taps, stamp_rows, stamp_cols):
    tap_count = col_taps.shape[1]
    margin = (tap_count - 1) // 2
    kernels = col_taps.shape[0]
    blocks = kernels // KBLK
    science_map = science[0]
    variance_map = variance[0]
    inverse = 1.0 / variance_map
    gathered = lax.all_gather(template, "visit", axis=0, tiled=True)
    padded_tile = with_halo(gathered, (("sky", 1),), margin)
    image_list = []
    for block_index in range(blocks):
        image_list.append(
            row_pass(
                column_pass(padded_tile, col_taps[block_index * KBLK : (block_index + 1) * KBLK]),
                row_taps[block_index * KBLK : (block_index + 1) * KBLK],
            )
        )
    convolved = jnp.concatenate(image_list, axis=0)
    row_starts = stamp_rows[0, 0]
    col_starts = stamp_cols[0, 0]
    design_core = extract_stamps(convolved, row_starts, col_starts)
    design = jnp.concatenate(
        [design_core, jnp.ones((1, design_core.shape[1]), design_core.dtype)], axis=0
    ).astype(jnp.float32)
    weights = 1.0 / extract_plane(variance_map, row_starts, col_starts)
    values = extract_plane(science_map, row_starts, col_starts)
    partial_normal = jnp.dot(design * weights[None, :], design.T, precision=lax.Precision.HIGHEST)
    partial_target = jnp.dot(design, weights * values, precision=lax.Precision.HIGHEST)
    normal, target = lax.psum((partial_normal, partial_target), "sky")
    solution = cholesky_solve(normal, target)

    def model_step(block_index, total):
        images = lax.dynamic_slice_in_dim(convolved, block_index * KBLK, KBLK, 0).astype(
            jnp.float32
        )
        share = lax.dynamic_slice_in_dim(solution, block_index * KBLK, KBLK, 0)
        return total + jnp.tensordot(share, images, axes=1, precision=lax.Precision.HIGHEST)

    model_map = lax.fori_loop(0, blocks, model_step, jnp.zeros(science_map.shape, jnp.float32))
    residual = science_map - model_map - solution[kernels]
    difference = (residual / jnp.sqrt(variance_map))[None, :, :]
    weighted = residual / variance_map
    numerator, weight_total = (
        lax.psum_scatter(weighted, "visit", scatter_dimension=0, tiled=True),
        lax.psum_scatter(inverse, "visit", scatter_dimension=0, tiled=True),
    )
    detection = numerator / jnp.sqrt(weight_total)
    return (difference, solution[None, :], detection)


MESH = pl.DeviceIdType.MESH
SUB = 8
OPERANDS = 7
RESULTS = 3
VMEM_BYTES = 60 * 2**20
EXTRA = 4


def dot(a, b, contract=((1,), (0,))):
    return lax.dot_general(a, b, (contract, ((), ())), preferred_element_type=jnp.float32)


def split3(value):
    high = value.astype(jnp.bfloat16)
    rest = value - high.astype(jnp.float32)
    middle = rest.astype(jnp.bfloat16)
    low = (rest - middle.astype(jnp.float32)).astype(jnp.bfloat16)
    return high, middle, low


def iota(shape, dim):
    return lax.broadcasted_iota(jnp.int32, shape, dim)


def placed_taps(taps, lanes, sign):
    count = taps.shape[0]
    margin = (count - 1) // 2
    spot = sign * (iota((count, lanes), 0) - margin)
    spot = jnp.where(spot < 0, spot + lanes, spot)
    place = jnp.where(iota((count, lanes), 1) == spot, 1.0, 0.0).astype(jnp.bfloat16)
    return dot(taps, place, ((0,), (0,)))


def reciprocal(value):
    guess = pl.reciprocal(value, approx=True)
    guess = guess * (2.0 - value * guess)
    return guess * (2.0 - value * guess)


def fused_kernel(
    n,
    *refs,
):
    operands, refs = refs[:OPERANDS], refs[OPERANDS:]
    results, refs = refs[:RESULTS], refs[RESULTS:]
    held, loaded, refs = refs[:OPERANDS], refs[OPERANDS], refs[OPERANDS + 1 :]
    ready, stored, refs = refs[:RESULTS], refs[RESULTS], refs[RESULTS + 1 :]
    stores = [
        pltpu.make_async_copy(here, result, stored.at[i])
        for i, (here, result) in enumerate(zip(ready, results))
    ]
    body(n, operands, held, loaded, stores, *ready, *refs)


def body(
    n,
    operands,
    held,
    loaded,
    stores,
    difference_ref,
    coefficients_ref,
    detection_ref,
    outbox,
    inbox,
    parts_out,
    parts_in,
    tile,
    col_bands,
    row_bands,
    design,
    send_a,
    recv_a,
    send_b,
    recv_b,
):
    template_ref, science_ref, variance_ref, col_taps_ref, row_taps_ref = held[:5]
    stamp_rows_ref, stamp_cols_ref = held[5:]
    me = lax.axis_index("visit")
    taps, kernels = col_taps_ref.shape
    margin = (taps - 1) // 2
    share, width = template_ref.shape
    height = science_ref.shape[1]
    groups = row_bands.shape[0]
    stacked = SUB * height

    def copies(source, target, send, recv):
        return [
            pltpu.make_async_remote_copy(
                src_ref=source.at[lax.rem(me + step, n)],
                dst_ref=target.at[me],
                send_sem=send.at[step],
                recv_sem=recv.at[step],
                device_id={"visit": lax.rem(me + step, n)},
                device_id_type=MESH,
            )
            for step in range(1, n)
        ]

    barrier = pltpu.get_barrier_semaphore()
    for step in range(1, n):
        pl.semaphore_signal(
            barrier, inc=1, device_id={"visit": lax.rem(me + step, n)}, device_id_type=MESH
        )

    fetches = [
        pltpu.make_async_copy(operand, here, loaded.at[i])
        for i, (operand, here) in enumerate(zip(operands, held))
    ]
    for fetch in fetches:
        fetch.start()
    for fetch in fetches[:3]:
        fetch.wait()

    science = science_ref[0]
    variance = variance_ref[0]
    inverse = 1.0 / variance
    own_rows = template_ref[...].astype(jnp.float32)
    for owner in range(n):
        outbox[owner, 0:share, :] = own_rows
        outbox[owner, share : 2 * share, :] = inverse[owner * share : (owner + 1) * share]
    inbox[me] = outbox[me]

    for fetch in fetches[3:]:
        fetch.wait()

    spread = placed_taps(row_taps_ref[...], width, 1)
    spread = jnp.concatenate(
        [spread, jnp.zeros((groups * SUB - kernels, width), jnp.float32)], axis=0
    )
    per_tile = width // height
    sub_of = iota((SUB, width), 0)
    for group in range(groups):
        source = spread[group * SUB : (group + 1) * SUB]
        base = source
        for slot in range(1, per_tile):
            base = jnp.where(sub_of % per_tile == slot, pltpu.roll(source, slot * height, 1), base)
        for row in range(0, height, 2):
            turned = [pltpu.roll(base, row + more, 1) for more in range(2)]
            for part in range(stacked // width):
                own = iota((SUB, width), 1) // height + part * per_tile == sub_of
                pair = [jnp.where(own, one, 0.0) for one in turned]
                row_bands[
                    group, row * SUB : (row + 2) * SUB, part * width : (part + 1) * width
                ] = jnp.concatenate(pair, axis=0).astype(jnp.bfloat16)

    pl.semaphore_wait(barrier, n - 1)
    first = copies(outbox, inbox, send_a, recv_a)
    for copy in first:
        copy.start()

    lanes = placed_taps(col_taps_ref[...], width, -1)
    near = jnp.abs(iota((width, width), 0) - iota((width, width), 1)) <= margin
    for k in range(kernels):
        base = pltpu.roll(
            jnp.broadcast_to(lanes[k : k + 1], (width, width)), 0, 1, stride=1, stride_axis=0
        )
        col_bands[:, k * width : (k + 1) * width] = jnp.where(near, base, 0.0).astype(jnp.bfloat16)

    tops = stamp_rows_ref[0]
    lefts = stamp_cols_ref[0]
    down = iota((height, tops.shape[1]), 0) - tops
    across = iota((width, lefts.shape[1]), 0) - lefts
    in_rows = jnp.where((down >= 0) & (down < STAMP), 1.0, 0.0).astype(jnp.bfloat16)
    in_cols = jnp.where((across >= 0) & (across < STAMP), 1.0, 0.0).astype(jnp.bfloat16)
    weights = dot(in_rows, in_cols, ((1,), (1,))) * inverse
    pieces = [p.astype(jnp.float32) for p in split3(science)]

    def constant_rows(group, row):
        block = jnp.zeros((SUB, width), jnp.float32)
        for extra in range(EXTRA):
            index = kernels + extra - group * SUB
            if 0 <= index < SUB:
                entry = (
                    jnp.ones((1, width), jnp.float32)
                    if extra == 0
                    else pieces[extra - 1][row : row + 1]
                )
                block = jnp.where(iota((SUB, width), 0) == index, entry, block)
        return block

    for copy in first:
        copy.wait_recv()
    for owner in range(n):
        tile[owner * share : (owner + 1) * share, :] = inbox[owner, 0:share, :]
    weight_total = inbox[0, share : 2 * share, :]
    for owner in range(1, n):
        weight_total = weight_total + inbox[owner, share : 2 * share, :]
    scale = jnp.sqrt(weight_total)

    columns = dot(tile[...].astype(jnp.bfloat16), col_bands[...]).astype(jnp.bfloat16)
    for group in range(groups):
        members = range(group * SUB, min((group + 1) * SUB, kernels))
        if len(members):
            block = jnp.concatenate([columns[:, k * width : (k + 1) * width] for k in members], 0)
            images = dot(row_bands[group, :, 0 : len(members) * height], block)
            images = images.astype(jnp.bfloat16).astype(jnp.float32)
        else:
            images = jnp.zeros((stacked, width), jnp.float32)
        for row in range(height):
            image = images[row * SUB : (row + 1) * SUB]
            if (group + 1) * SUB > kernels:
                image = image + constant_rows(group, row)
            design[row, group * SUB : (group + 1) * SUB, :] = image

    flat = jnp.concatenate([design[row] for row in range(height)], axis=1)
    flat_weights = jnp.concatenate([weights[row : row + 1] for row in range(height)], axis=1)
    gap = jnp.zeros((-flat.shape[0] % 16, flat.shape[1]), jnp.float32)
    flat = jnp.concatenate([flat, gap], axis=0)
    left = jnp.concatenate(split3(flat * flat_weights), axis=0)
    grams = dot(left, flat.astype(jnp.bfloat16), ((1,), (1,)))
    size = flat.shape[0]
    gram = grams[0:size] + grams[size : 2 * size] + grams[2 * size : 3 * size]
    gram = gram[0 : groups * SUB]
    unknowns = kernels + 1
    target = gram[:, unknowns : unknowns + 1]
    for extra in range(2, EXTRA):
        target = target + gram[:, kernels + extra : kernels + extra + 1]
    gram = jnp.where(iota(gram.shape, 1) == unknowns, target, gram)

    parts = [gram[g * SUB : (g + 1) * SUB] for g in range(groups)]
    shape = parts[0].shape
    subs = iota(shape, 0)
    lane = iota(shape, 1)
    on_diagonal = [(lane == subs + g * SUB) & (lane < unknowns) for g in range(groups)]
    diagonals = [jnp.where(on_diagonal[g], parts[g], 0.0) for g in range(groups)]
    along = jnp.sum(functools.reduce(jnp.add, diagonals), axis=0, keepdims=True)
    along = lax.rsqrt(jnp.where(iota(along.shape, 1) < unknowns, along, 1.0))
    down_scales = []
    for g in range(groups):
        entry = jnp.sum(diagonals[g], axis=1, keepdims=True)
        entry = jnp.where(iota(entry.shape, 0) + g * SUB < unknowns, entry, 1.0)
        down_scales.append(lax.rsqrt(jnp.broadcast_to(entry, shape)))
    system = [parts[g] * along * down_scales[g] for g in range(groups)]
    for home in range(groups):
        begin = home * SUB
        size = min(SUB, unknowns - begin)
        if size <= 0:
            break
        rows = [jnp.broadcast_to(system[home][s : s + 1], shape) for s in range(size)]
        own_factors = [
            jnp.broadcast_to(system[home][:, begin + s : begin + s + 1], shape)
            for s in range(size)
        ]
        upper = {
            (t, u): jnp.broadcast_to(own_factors[u][t : t + 1], shape)
            for t in range(size)
            for u in range(t, size)
        }
        steps = []
        for s in range(0, size, 2):
            later = range(s + 2, size)
            if s + 1 < size:
                a, b, c = upper[s, s], upper[s, s + 1], upper[s + 1, s + 1]
                det = reciprocal(a * c - b * b)
                aa, bb, cc = c * det, -b * det, a * det
                first_by = {u: aa * upper[s, u] + bb * upper[s + 1, u] for u in later}
                second_by = {u: bb * upper[s, u] + cc * upper[s + 1, u] for u in later}
                for t in later:
                    for u in range(t, size):
                        upper[t, u] = upper[t, u] - (
                            upper[s, t] * first_by[u] + upper[s + 1, t] * second_by[u]
                        )
                rows[s], rows[s + 1] = (
                    aa * rows[s] + bb * rows[s + 1],
                    bb * rows[s] + cc * rows[s + 1],
                )
                for t in later:
                    rows[t] = rows[t] - (upper[s, t] * rows[s] + upper[s + 1, t] * rows[s + 1])
                steps += [(s, first_by), (s + 1, second_by)]
            else:
                rows[s] = rows[s] * reciprocal(upper[s, s])
        for s, by in reversed(steps):
            for u, value in by.items():
                rows[s] = rows[s] - value * rows[u]
        for g in range(groups):
            if g == home:
                for s in range(size):
                    system[g] = jnp.where(subs == s, rows[s], system[g])
                continue
            change = None
            for s in range(size):
                factor = jnp.broadcast_to(system[g][:, begin + s : begin + s + 1], shape)
                change = factor * rows[s] if change is None else change + factor * rows[s]
            system[g] = system[g] - change
    system = [system[g] * down_scales[g] for g in range(groups)]
    answers = [
        jnp.where(
            iota((SUB, width), 0) + g * SUB < unknowns,
            jnp.broadcast_to(system[g][:, unknowns : unknowns + 1], (SUB, width)),
            0.0,
        )
        for g in range(groups)
    ]
    answer = jnp.concatenate(answers, axis=0)

    model = jnp.sum(design[...] * answer[None], axis=1)
    residual = science - model
    weighted = residual * inverse
    for owner in range(n):
        parts_out[owner] = weighted[owner * share : (owner + 1) * share]
    parts_in[me] = parts_out[me]
    second = copies(parts_out, parts_in, send_b, recv_b)
    for copy in second:
        copy.start()

    difference_ref[0] = residual / jnp.sqrt(variance)
    across = jnp.sum(
        jnp.where(iota(answer.shape, 0) == iota(answer.shape, 1), answer, 0.0), axis=0, keepdims=True
    )
    coefficients_ref[...] = across[:, 0:unknowns]
    for store in stores[:-1]:
        store.start()

    for copy in second:
        copy.wait_recv()
    numerator = parts_in[0]
    for owner in range(1, n):
        numerator = numerator + parts_in[owner]
    detection_ref[...] = numerator / scale
    stores[-1].start()
    for copy in first + second:
        copy.wait_send()
    for store in stores:
        store.wait()


def hand_over(*refs):
    done = refs[-1]
    moves = [
        pltpu.make_async_copy(refs[i], refs[RESULTS + i], done.at[i]) for i in range(RESULTS)
    ]
    for move in moves:
        move.start()
    for move in moves:
        move.wait()


def fused(n, template, science, variance, col_taps, row_taps, stamp_rows, stamp_cols):
    kernels = col_taps.shape[0]
    share, width = template.shape
    height = science.shape[1]
    groups = -(-(kernels + EXTRA) // SUB)
    stacked = SUB * height
    hbm = pl.BlockSpec(memory_space=pltpu.HBM)
    operands = (template, science, variance, col_taps.T, row_taps.T, stamp_rows, stamp_cols)
    shapes = (
        jax.ShapeDtypeStruct(science.shape, jnp.float32),
        jax.ShapeDtypeStruct((1, kernels + 1), jnp.float32),
        jax.ShapeDtypeStruct((share, width), jnp.float32),
    )
    results = pl.pallas_call(
        functools.partial(fused_kernel, n),
        out_shape=shapes,
        in_specs=[hbm] * OPERANDS,
        out_specs=(hbm,) * RESULTS,
        scratch_shapes=[pltpu.VMEM(operand.shape, operand.dtype) for operand in operands]
        + [
            pltpu.SemaphoreType.DMA((OPERANDS,)),
        ]
        + [pltpu.VMEM(shape.shape, shape.dtype) for shape in shapes]
        + [
            pltpu.SemaphoreType.DMA((RESULTS,)),
            pltpu.VMEM((n, 2 * share, width), jnp.float32),
            pltpu.VMEM((n, 2 * share, width), jnp.float32),
            pltpu.VMEM((n, share, width), jnp.float32),
            pltpu.VMEM((n, share, width), jnp.float32),
            pltpu.VMEM((height, width), jnp.float32),
            pltpu.VMEM((width, kernels * width), jnp.bfloat16),
            pltpu.VMEM((groups, stacked, stacked), jnp.bfloat16),
            pltpu.VMEM((height, groups * SUB, width), jnp.float32),
            pltpu.SemaphoreType.DMA((n,)),
            pltpu.SemaphoreType.DMA((n,)),
            pltpu.SemaphoreType.DMA((n,)),
            pltpu.SemaphoreType.DMA((n,)),
        ],
        compiler_params=pltpu.CompilerParams(
            collective_id=0, has_side_effects=True, vmem_limit_bytes=VMEM_BYTES
        ),
    )(*operands)
    return pl.pallas_call(
        hand_over,
        out_shape=shapes,
        in_specs=[hbm] * RESULTS,
        out_specs=(hbm,) * RESULTS,
        scratch_shapes=[pltpu.SemaphoreType.DMA((RESULTS,))],
        compiler_params=pltpu.CompilerParams(vmem_limit_bytes=VMEM_BYTES),
    )(*results)


def per_device(axes, template, science, *rest):
    height, width = science.shape[1:]
    if axes["sky"] == 1 and width % 128 == 0 and SUB * height == 2 * width:
        return fused(axes["visit"], template, science, *rest)
    return on_device(template, science, *rest)


def solution(mesh):
    in_specs = (
        P(("group", "visit"), "sky"),
        P(("group", "visit"), None, "sky"),
        P(("group", "visit"), None, "sky"),
        P(),
        P(),
        P(("group", "visit"), "sky", None),
        P(("group", "visit"), "sky", None),
    )
    out_specs = (
        P(("group", "visit"), None, "sky"),
        P(("group", "visit"), None),
        P(("group", "visit"), "sky"),
    )
    return jax.shard_map(
        functools.partial(per_device, dict(mesh.shape)), mesh=mesh, in_specs=in_specs, out_specs=out_specs, check_vma=False
    )
```

```python
import functools

import jax
import jax.numpy as jnp
from jax import lax
from jax.experimental import pallas as pl
from jax.experimental.pallas import tpu as pltpu
from jax.sharding import PartitionSpec as P

KBLK = 7
STAMP = 16


def with_halo(cells, sides, width):
    for axis, dim in sides:
        count = lax.axis_size(axis)
        ends = count - 1
        head = lax.slice_in_dim(cells, 0, width, axis=dim)
        tail = lax.slice_in_dim(cells, cells.shape[dim] - width, cells.shape[dim], axis=dim)
        cells = jnp.concatenate(
            [
                lax.ppermute(tail, axis, [(i, (i + 1) % count) for i in range(ends)]),
                cells,
                lax.ppermute(head, axis, [((i + 1) % count, i) for i in range(ends)]),
            ],
            axis=dim,
        )
    return cells


def tap_selectors(out_len, in_len, tap_count):
    offsets = (
        jnp.arange(in_len, dtype=jnp.int32)[None, :] - jnp.arange(out_len, dtype=jnp.int32)[:, None]
    )
    return (offsets[None, :, :] == jnp.arange(tap_count, dtype=jnp.int32)[:, None, None]).astype(
        jnp.float32
    )


def column_pass(padded, taps_block):
    tap_count = taps_block.shape[1]
    out_width = padded.shape[1] - tap_count + 1
    selectors = tap_selectors(out_width, padded.shape[1], tap_count)
    band_mats = jnp.einsum("kj,jci->kic", taps_block.astype(jnp.float32), selectors).astype(
        jnp.bfloat16
    )
    result = jnp.einsum("ri,kic->krc", padded, band_mats, preferred_element_type=jnp.float32)
    return result.astype(jnp.bfloat16)


def band_matrix(taps_block, out_len, in_len):
    tap_count = taps_block.shape[1]
    offsets = (
        jnp.arange(in_len, dtype=jnp.int32)[None, :] - jnp.arange(out_len, dtype=jnp.int32)[:, None]
    )
    taps_wide = taps_block.astype(jnp.float32)
    band = jnp.zeros((taps_block.shape[0], out_len, in_len), jnp.float32)
    for offset in range(tap_count):
        band = band + jnp.where(
            offsets[None, :, :] == offset, taps_wide[:, offset][:, None, None], 0.0
        )
    return band.astype(jnp.bfloat16)


def row_pass(columns, taps_block):
    tap_count = taps_block.shape[1]
    margin = (tap_count - 1) // 2
    height = columns.shape[1]
    stride = min(512, height)
    padded = jnp.pad(columns, ((0, 0), (margin, margin), (0, 0)))
    band = band_matrix(taps_block, stride, stride + 2 * margin)
    pieces = jnp.einsum("kti,kiw->ktw", band, padded, preferred_element_type=jnp.float32).astype(
        jnp.bfloat16
    )
    return pieces


def extract_stamps(block, row_starts, col_starts):

    def extract(row_start, col_start):
        return lax.dynamic_slice(
            block, (jnp.int32(0), row_start, col_start), (block.shape[0], STAMP, STAMP)
        )

    stamps = jax.vmap(extract)(row_starts, col_starts)
    return jnp.transpose(stamps, (1, 0, 2, 3)).reshape(block.shape[0], -1)


def extract_plane(plane, row_starts, col_starts):

    def extract(row_start, col_start):
        return lax.dynamic_slice(plane, (row_start, col_start), (STAMP, STAMP))

    return jax.vmap(extract)(row_starts, col_starts).reshape(-1)


def cholesky_solve(matrix, vector):
    factor = jnp.linalg.cholesky(matrix)
    middle = lax.linalg.triangular_solve(factor, vector[:, None], left_side=True, lower=True)
    answer = lax.linalg.triangular_solve(
        factor, middle, left_side=True, lower=True, transpose_a=True
    )
    return answer[:, 0]


def on_device(template, science, variance, col_taps, row_taps, stamp_rows, stamp_cols):
    tap_count = col_taps.shape[1]
    margin = (tap_count - 1) // 2
    kernels = col_taps.shape[0]
    blocks = kernels // KBLK
    science_map = science[0]
    variance_map = variance[0]
    inverse = 1.0 / variance_map
    gathered = lax.all_gather(template, "visit", axis=0, tiled=True)
    padded_tile = with_halo(gathered, (("sky", 1),), margin)
    image_list = []
    for block_index in range(blocks):
        image_list.append(
            row_pass(
                column_pass(padded_tile, col_taps[block_index * KBLK : (block_index + 1) * KBLK]),
                row_taps[block_index * KBLK : (block_index + 1) * KBLK],
            )
        )
    convolved = jnp.concatenate(image_list, axis=0)
    row_starts = stamp_rows[0, 0]
    col_starts = stamp_cols[0, 0]
    design_core = extract_stamps(convolved, row_starts, col_starts)
    design = jnp.concatenate(
        [design_core, jnp.ones((1, design_core.shape[1]), design_core.dtype)], axis=0
    ).astype(jnp.float32)
    weights = 1.0 / extract_plane(variance_map, row_starts, col_starts)
    values = extract_plane(science_map, row_starts, col_starts)
    partial_normal = jnp.dot(design * weights[None, :], design.T, precision=lax.Precision.HIGHEST)
    partial_target = jnp.dot(design, weights * values, precision=lax.Precision.HIGHEST)
    normal, target = lax.psum((partial_normal, partial_target), "sky")
    solution = cholesky_solve(normal, target)

    def model_step(block_index, total):
        images = lax.dynamic_slice_in_dim(convolved, block_index * KBLK, KBLK, 0).astype(
            jnp.float32
        )
        share = lax.dynamic_slice_in_dim(solution, block_index * KBLK, KBLK, 0)
        return total + jnp.tensordot(share, images, axes=1, precision=lax.Precision.HIGHEST)

    model_map = lax.fori_loop(0, blocks, model_step, jnp.zeros(science_map.shape, jnp.float32))
    residual = science_map - model_map - solution[kernels]
    difference = (residual / jnp.sqrt(variance_map))[None, :, :]
    weighted = residual / variance_map
    numerator, weight_total = (
        lax.psum_scatter(weighted, "visit", scatter_dimension=0, tiled=True),
        lax.psum_scatter(inverse, "visit", scatter_dimension=0, tiled=True),
    )
    detection = numerator / jnp.sqrt(weight_total)
    return (difference, solution[None, :], detection)


MESH = pl.DeviceIdType.MESH
SUB = 8
RESULTS = 3
VMEM_BYTES = 16 * 2**20
EXTRA = 4


def dot(a, b, contract=((1,), (0,))):
    return lax.dot_general(a, b, (contract, ((), ())), preferred_element_type=jnp.float32)


def split3(value):
    high = value.astype(jnp.bfloat16)
    rest = value - high.astype(jnp.float32)
    middle = rest.astype(jnp.bfloat16)
    low = (rest - middle.astype(jnp.float32)).astype(jnp.bfloat16)
    return high, middle, low


def iota(shape, dim):
    return lax.broadcasted_iota(jnp.int32, shape, dim)


def placed_taps(taps, lanes, sign):
    count = taps.shape[1]
    margin = (count - 1) // 2
    spot = sign * (iota((count, lanes), 0) - margin)
    spot = jnp.where(spot < 0, spot + lanes, spot)
    place = jnp.where(iota((count, lanes), 1) == spot, 1.0, 0.0).astype(jnp.bfloat16)
    return dot(taps, place)


def fused_kernel(
    n,
    template_ref,
    science_ref,
    variance_ref,
    col_taps_ref,
    row_taps_ref,
    stamp_rows_ref,
    stamp_cols_ref,
    difference_ref,
    coefficients_ref,
    detection_ref,
    outbox,
    inbox,
    parts_out,
    parts_in,
    tile,
    col_bands,
    row_bands,
    design,
    send_a,
    recv_a,
    send_b,
    recv_b,
):
    me = lax.axis_index("visit")
    kernels, taps = col_taps_ref.shape
    margin = (taps - 1) // 2
    share, width = template_ref.shape
    height = science_ref.shape[1]
    groups = row_bands.shape[0]
    stacked = SUB * height

    def copies(source, target, send, recv):
        return [
            pltpu.make_async_remote_copy(
                src_ref=source.at[lax.rem(me + step, n)],
                dst_ref=target.at[me],
                send_sem=send.at[step],
                recv_sem=recv.at[step],
                device_id={"visit": lax.rem(me + step, n)},
                device_id_type=MESH,
            )
            for step in range(1, n)
        ]

    barrier = pltpu.get_barrier_semaphore()
    for step in range(1, n):
        pl.semaphore_signal(
            barrier, inc=1, device_id={"visit": lax.rem(me + step, n)}, device_id_type=MESH
        )

    science = science_ref[0]
    variance = variance_ref[0]
    inverse = 1.0 / variance
    own_rows = template_ref[...].astype(jnp.float32)
    for owner in range(n):
        outbox[owner, 0:share, :] = own_rows
        outbox[owner, share : 2 * share, :] = inverse[owner * share : (owner + 1) * share]
    inbox[me] = outbox[me]

    spread = placed_taps(row_taps_ref[...], width, 1)
    spread = jnp.concatenate(
        [spread, jnp.zeros((groups * SUB - kernels, width), jnp.float32)], axis=0
    )
    per_tile = width // height
    sub_of = iota((SUB, width), 0)
    for group in range(groups):
        source = spread[group * SUB : (group + 1) * SUB]
        base = source
        for slot in range(1, per_tile):
            base = jnp.where(sub_of % per_tile == slot, pltpu.roll(source, slot * height, 1), base)
        for row in range(0, height, 2):
            turned = [pltpu.roll(base, row + more, 1) for more in range(2)]
            for part in range(stacked // width):
                own = iota((SUB, width), 1) // height + part * per_tile == sub_of
                pair = [jnp.where(own, one, 0.0) for one in turned]
                row_bands[
                    group, row * SUB : (row + 2) * SUB, part * width : (part + 1) * width
                ] = jnp.concatenate(pair, axis=0).astype(jnp.bfloat16)

    pl.semaphore_wait(barrier, n - 1)
    first = copies(outbox, inbox, send_a, recv_a)
    for copy in first:
        copy.start()

    lanes = placed_taps(col_taps_ref[...], width, -1)
    near = jnp.abs(iota((width, width), 0) - iota((width, width), 1)) <= margin
    for k in range(kernels):
        base = pltpu.roll(
            jnp.broadcast_to(lanes[k : k + 1], (width, width)), 0, 1, stride=1, stride_axis=0
        )
        col_bands[:, k * width : (k + 1) * width] = jnp.where(near, base, 0.0).astype(jnp.bfloat16)

    tops = stamp_rows_ref[0]
    lefts = stamp_cols_ref[0]
    down = iota((height, tops.shape[1]), 0) - tops
    across = iota((width, lefts.shape[1]), 0) - lefts
    in_rows = jnp.where((down >= 0) & (down < STAMP), 1.0, 0.0).astype(jnp.bfloat16)
    in_cols = jnp.where((across >= 0) & (across < STAMP), 1.0, 0.0).astype(jnp.bfloat16)
    weights = dot(in_rows, in_cols, ((1,), (1,))) * inverse
    pieces = [p.astype(jnp.float32) for p in split3(science)]

    def constant_rows(group, row):
        block = jnp.zeros((SUB, width), jnp.float32)
        for extra in range(EXTRA):
            index = kernels + extra - group * SUB
            if 0 <= index < SUB:
                entry = (
                    jnp.ones((1, width), jnp.float32)
                    if extra == 0
                    else pieces[extra - 1][row : row + 1]
                )
                block = jnp.where(iota((SUB, width), 0) == index, entry, block)
        return block

    for copy in first:
        copy.wait_recv()
    for owner in range(n):
        tile[owner * share : (owner + 1) * share, :] = inbox[owner, 0:share, :]
    weight_total = inbox[0, share : 2 * share, :]
    for owner in range(1, n):
        weight_total = weight_total + inbox[owner, share : 2 * share, :]
    scale = jnp.sqrt(weight_total)

    columns = dot(tile[...].astype(jnp.bfloat16), col_bands[...]).astype(jnp.bfloat16)
    for group in range(groups):
        members = range(group * SUB, min((group + 1) * SUB, kernels))
        if len(members):
            block = jnp.concatenate([columns[:, k * width : (k + 1) * width] for k in members], 0)
            images = dot(row_bands[group, :, 0 : len(members) * height], block)
            images = images.astype(jnp.bfloat16).astype(jnp.float32)
        else:
            images = jnp.zeros((stacked, width), jnp.float32)
        for row in range(height):
            image = images[row * SUB : (row + 1) * SUB]
            if (group + 1) * SUB > kernels:
                image = image + constant_rows(group, row)
            design[row, group * SUB : (group + 1) * SUB, :] = image

    flat = jnp.concatenate([design[row] for row in range(height)], axis=1)
    flat_weights = jnp.concatenate([weights[row : row + 1] for row in range(height)], axis=1)
    gap = jnp.zeros((-flat.shape[0] % 16, flat.shape[1]), jnp.float32)
    flat = jnp.concatenate([flat, gap], axis=0)
    left = jnp.concatenate(split3(flat * flat_weights), axis=0)
    grams = dot(left, flat.astype(jnp.bfloat16), ((1,), (1,)))
    size = flat.shape[0]
    gram = grams[0:size] + grams[size : 2 * size] + grams[2 * size : 3 * size]
    gram = gram[0 : groups * SUB]
    unknowns = kernels + 1
    target = gram[:, unknowns : unknowns + 1]
    for extra in range(2, EXTRA):
        target = target + gram[:, kernels + extra : kernels + extra + 1]
    gram = jnp.where(iota(gram.shape, 1) == unknowns, target, gram)

    system = [gram[g * SUB : (g + 1) * SUB] for g in range(groups)]
    shape = system[0].shape
    subs = iota(shape, 0)
    for home in range(groups):
        begin = home * SUB
        size = min(SUB, unknowns - begin)
        if size <= 0:
            break
        factors = [
            [jnp.broadcast_to(part[:, begin + s : begin + s + 1], shape) for s in range(size)]
            for part in system
        ]
        rows = [jnp.broadcast_to(system[home][s : s + 1], shape) for s in range(size)]
        pivots = [
            [jnp.broadcast_to(factors[home][s][t : t + 1], shape) for s in range(size)]
            for t in range(size)
        ]
        for s in range(size):
            scale_by = 1.0 / pivots[s][s]
            for u in range(s + 1, size):
                pivots[s][u] = pivots[s][u] * scale_by
            rows[s] = rows[s] * scale_by
            for t in range(size):
                if t == s:
                    continue
                by = pivots[t][s]
                for u in range(s + 1, size):
                    pivots[t][u] = pivots[t][u] - by * pivots[s][u]
                rows[t] = rows[t] - by * rows[s]
        for g in range(groups):
            if g == home:
                for s in range(size):
                    system[g] = jnp.where(subs == s, rows[s], system[g])
                continue
            change = factors[g][0] * rows[0]
            for s in range(1, size):
                change = change + factors[g][s] * rows[s]
            system[g] = system[g] - change
    answers = [
        jnp.where(
            iota((SUB, width), 0) + g * SUB < unknowns,
            jnp.broadcast_to(system[g][:, unknowns : unknowns + 1], (SUB, width)),
            0.0,
        )
        for g in range(groups)
    ]
    answer = jnp.concatenate(answers, axis=0)

    model = jnp.sum(design[...] * answer[None], axis=1)
    residual = science - model
    weighted = residual * inverse
    for owner in range(n):
        parts_out[owner] = weighted[owner * share : (owner + 1) * share]
    parts_in[me] = parts_out[me]
    second = copies(parts_out, parts_in, send_b, recv_b)
    for copy in second:
        copy.start()

    difference_ref[0] = residual / jnp.sqrt(variance)
    across = jnp.sum(
        jnp.where(iota(answer.shape, 0) == iota(answer.shape, 1), answer, 0.0), axis=0, keepdims=True
    )
    coefficients_ref[...] = across[:, 0:unknowns]

    for copy in second:
        copy.wait_recv()
    numerator = parts_in[0]
    for owner in range(1, n):
        numerator = numerator + parts_in[owner]
    detection_ref[...] = numerator / scale
    for copy in first + second:
        copy.wait_send()


def hand_over(*refs):
    done = refs[-1]
    moves = [
        pltpu.make_async_copy(refs[i], refs[RESULTS + i], done.at[i]) for i in range(RESULTS)
    ]
    for move in moves:
        move.start()
    for move in moves:
        move.wait()


def fused(n, template, science, variance, col_taps, row_taps, stamp_rows, stamp_cols):
    kernels = col_taps.shape[0]
    share, width = template.shape
    height = science.shape[1]
    groups = -(-(kernels + EXTRA) // SUB)
    stacked = SUB * height
    vmem = pl.BlockSpec(memory_space=pltpu.VMEM)
    hbm = pl.BlockSpec(memory_space=pltpu.HBM)
    operands = (template, science, variance, col_taps, row_taps, stamp_rows, stamp_cols)
    shapes = (
        jax.ShapeDtypeStruct(science.shape, jnp.float32),
        jax.ShapeDtypeStruct((1, kernels + 1), jnp.float32),
        jax.ShapeDtypeStruct((share, width), jnp.float32),
    )
    results = pl.pallas_call(
        functools.partial(fused_kernel, n),
        out_shape=shapes,
        in_specs=[vmem] * len(operands),
        out_specs=(vmem,) * RESULTS,
        scratch_shapes=[
            pltpu.VMEM((n, 2 * share, width), jnp.float32),
            pltpu.VMEM((n, 2 * share, width), jnp.float32),
            pltpu.VMEM((n, share, width), jnp.float32),
            pltpu.VMEM((n, share, width), jnp.float32),
            pltpu.VMEM((height, width), jnp.float32),
            pltpu.VMEM((width, kernels * width), jnp.bfloat16),
            pltpu.VMEM((groups, stacked, stacked), jnp.bfloat16),
            pltpu.VMEM((height, groups * SUB, width), jnp.float32),
            pltpu.SemaphoreType.DMA((n,)),
            pltpu.SemaphoreType.DMA((n,)),
            pltpu.SemaphoreType.DMA((n,)),
            pltpu.SemaphoreType.DMA((n,)),
        ],
        compiler_params=pltpu.CompilerParams(
            collective_id=0, has_side_effects=True, vmem_limit_bytes=VMEM_BYTES
        ),
    )(*operands)
    return pl.pallas_call(
        hand_over,
        out_shape=shapes,
        in_specs=[vmem] * RESULTS,
        out_specs=(hbm,) * RESULTS,
        scratch_shapes=[pltpu.SemaphoreType.DMA((RESULTS,))],
        compiler_params=pltpu.CompilerParams(vmem_limit_bytes=VMEM_BYTES),
    )(*results)


def per_device(axes, template, science, *rest):
    height, width = science.shape[1:]
    if axes["sky"] == 1 and width % 128 == 0 and SUB * height == 2 * width:
        return fused(axes["visit"], template, science, *rest)
    return on_device(template, science, *rest)


def solution(mesh):
    in_specs = (
        P(("group", "visit"), "sky"),
        P(("group", "visit"), None, "sky"),
        P(("group", "visit"), None, "sky"),
        P(),
        P(),
        P(("group", "visit"), "sky", None),
        P(("group", "visit"), "sky", None),
    )
    out_specs = (
        P(("group", "visit"), None, "sky"),
        P(("group", "visit"), None),
        P(("group", "visit"), "sky"),
    )
    return jax.shard_map(
        functools.partial(per_device, dict(mesh.shape)), mesh=mesh, in_specs=in_specs, out_specs=out_specs, check_vma=False
    )
```
